32 devices in a mesh: rep: 2 (over y), dom: 16 (over z, x, core).
Axes of the slice: x: 2, y: 2, z: 4, core: 2. Of those that a mesh axis runs over, the one named last changes fastest.
Arguments:
- feats: bfloat16 [4096, 256], P(('rep', 'dom')), may hold values from -6 to 6
- w_self: bfloat16 [256, 256], replicated, may hold values from -0.375 to 0.375
- w_neigh: bfloat16 [256, 256], replicated, may hold values from -1.5 to 1.5
- tile_vals: bfloat16 [2, 16, 8, 128, 128], P('rep', 'dom'), may hold values from 0 to 1
- tile_owner: int32 [2, 16, 8], P('rep', 'dom'), may hold values from 0 to 15, as said below
- tile_src: int32 [2, 16, 8], P('rep', 'dom'), may hold values from 0 to 1
- tile_count: int32 [2, 16], P('rep', 'dom'), may hold values from 4 to 8, as said below
- d_out: bfloat16 [4096, 256], P(('rep', 'dom')), may hold values from -6 to 6
Outputs:
- out_feats: bfloat16 [4096, 256], P(('rep', 'dom'))
- d_feats: bfloat16 [4096, 256], P(('rep', 'dom'))
- grad_self: float32 [256, 256], P('dom')
- grad_neigh: float32 [256, 256], P('dom')
The draws below stay inside these ranges and needn't reach their ends.
Inputs may be any that keep to these rules, and one draw needn't show every extreme that they name: Within one list no two tiles name the same pair of tile_owner and tile_src. Tiles of list (i, j) at positions tile_count[i, j] and beyond are padding.
All inputs are finite; a program needn't handle non-finite values.
Results may differ from the reference program's by a relative error of at most 0.0049.
Values may be sent and summed in bfloat16 or wider, within the bound.
A program may use at most 128 MiB of HBM per device.

```python
import jax
import jax.numpy as jnp
from jax import lax

HID = 256
TILE = 128
ROWS = 128
TILES = 8
NODES = 4096
N_REP = 2
N_DOM = 16


def tile_places(key):
    per_block = ROWS // TILE
    total = N_DOM * per_block * N_REP * per_block
    keys = jax.random.split(jax.random.fold_in(key, 7), N_REP * N_DOM)
    picked = jax.vmap(lambda one_key: jax.random.permutation(one_key, total)[:TILES])(keys)
    return picked.reshape(N_REP, N_DOM, TILES).astype(jnp.int32)


def draw_tile_owner(key, part):
    return (tile_places(key) // (N_REP * (ROWS // TILE))).astype(jnp.int32)


def draw_tile_src(key, part):
    return (tile_places(key) % (N_REP * (ROWS // TILE))).astype(jnp.int32)


def draw_tile_count(key, part):
    keys = jax.random.split(jax.random.fold_in(key, 11), 3)
    lists = N_REP * N_DOM
    lowest = max(TILES // 2, 1)
    spread = jax.random.randint(keys[0], (lists,), lowest, TILES + 1)
    chosen = jax.random.randint(keys[1], (), 0, lists)
    second = (chosen + 1 + jax.random.randint(keys[2], (), 0, lists - 1)) % lists
    positions = jnp.arange(lists)
    filled = jnp.where(positions == chosen, TILES, jnp.where(positions == second, lowest, spread))
    return filled.reshape(N_REP, N_DOM).astype(jnp.int32)


def shard_levels(own_key, extent, pieces, low, top_value):
    def one(axis_at, blocks):
        heights = jax.random.uniform(jax.random.fold_in(jax.random.fold_in(own_key, 6), axis_at), (blocks,), jnp.float32, low / len(pieces), top_value / len(pieces))
        return jnp.repeat(jnp.exp(heights), extent[axis_at] // blocks).reshape((-1,) + (1,) * (len(extent) - axis_at - 1))

    gain = one(*pieces[0])
    for cut in pieces[1:]:
        gain = gain * one(*cut)
    return gain


def gaussian(own_key, extent, scale, reach, cuts=(), kind=jnp.bfloat16):
    gain = shard_levels(own_key, extent, cuts, -0.22, 0.18) if cuts else 1.0
    result = jax.random.normal(own_key, extent, jnp.float32) * scale * gain
    return jnp.minimum(jnp.maximum(result, -reach), reach).astype(kind)


def setup_inputs(seed: int = 0) -> dict:
    key_list = jax.random.split(jax.random.key(seed), 9)
    return {
        "feats": gaussian(key_list[0], (NODES, HID), 1.0, 6.0, ((0, 32),)),
        "w_self": gaussian(key_list[1], (HID, HID), HID ** -0.5, 0.375),
        "w_neigh": gaussian(key_list[2], (HID, HID), (HID // 16) ** -0.5, 1.5),
        "tile_vals": jnp.clip(1.0 * jax.random.uniform(key_list[3], (N_REP, N_DOM, TILES, TILE, TILE), jnp.float32) ** shard_levels(key_list[3], (N_REP, N_DOM, TILES, TILE, TILE), ((0, 2), (1, 16)), -0.2, 0.2), 0.0, 1.0).astype(jnp.bfloat16),
        "tile_owner": draw_tile_owner(jax.random.fold_in(key_list[8], 71), 0),
        "tile_src": draw_tile_src(jax.random.fold_in(key_list[8], 71), 0),
        "tile_count": draw_tile_count(jax.random.fold_in(key_list[8], 71), 0),
        "d_out": gaussian(key_list[7], (NODES, HID), 1.0, 6.0, ((0, 32),)),
    }


def reference(feats, w_self, w_neigh, tile_vals, tile_owner, tile_src, tile_count, d_out):
    per_block = ROWS // TILE
    hidden = feats.shape[1]
    lists = N_REP * N_DOM
    flat_vals = tile_vals.reshape(lists, TILES, TILE, TILE)
    flat_owner = tile_owner.reshape(lists, TILES)
    flat_src = tile_src.reshape(lists, TILES)
    flat_count = tile_count.reshape(lists)
    list_ids = jnp.arange(lists, dtype=jnp.int32)
    feat_tiles = feats.reshape(NODES // TILE, TILE, hidden)

    def placement(list_id, owners, sources, live_count):
        rep_id = list_id // N_DOM
        dom_id = list_id % N_DOM
        dest_rows = (rep_id * (N_DOM * per_block) + owners).astype(jnp.int32)
        src_rows = (((sources // per_block) * N_DOM + dom_id) * per_block + sources % per_block).astype(jnp.int32)
        live_mask = (jnp.arange(TILES, dtype=jnp.int32) < live_count).astype(jnp.float32)
        return dest_rows, src_rows, live_mask

    def forward_list(state_pair, inputs):
        neigh_sum, degree_sum = state_pair
        list_id, tile_block, owners, sources, live_count = inputs
        dest_rows, src_rows, live_mask = placement(list_id, owners, sources, live_count)
        block_f = tile_block.astype(jnp.float32)
        product = jnp.einsum("tij,tjc->tic", block_f, feat_tiles[src_rows].astype(jnp.float32), precision=lax.Precision.HIGHEST)
        neigh_sum = neigh_sum.at[dest_rows].add(product * live_mask[:, None, None])
        degree_sum = degree_sum.at[dest_rows].add(jnp.sum(block_f, axis=2) * live_mask[:, None])
        return (neigh_sum, degree_sum), None

    start_sum = jnp.zeros((NODES // TILE, TILE, hidden), jnp.float32)
    start_deg = jnp.zeros((NODES // TILE, TILE), jnp.float32)
    (neigh_sum, degree_sum), _ = lax.scan(forward_list, (start_sum, start_deg), (list_ids, flat_vals, flat_owner, flat_src, flat_count))
    degree = 1.0 + degree_sum.reshape(NODES)
    mean_agg = (neigh_sum.reshape(NODES, hidden) / degree[:, None]).astype(jnp.bfloat16)
    pre_act = jnp.dot(feats, w_self, preferred_element_type=jnp.float32) + jnp.dot(mean_agg, w_neigh, preferred_element_type=jnp.float32)
    sigmoid_pre = jax.nn.sigmoid(pre_act)
    out_feats = (pre_act * sigmoid_pre).astype(jnp.bfloat16)
    d_pre = (d_out.astype(jnp.float32) * sigmoid_pre * (1.0 + pre_act * (1.0 - sigmoid_pre))).astype(jnp.bfloat16)
    grad_self = jnp.dot(feats.T, d_pre, preferred_element_type=jnp.float32)
    grad_neigh = jnp.dot(mean_agg.T, d_pre, preferred_element_type=jnp.float32)
    d_sum = (jnp.dot(d_pre, w_neigh.T, preferred_element_type=jnp.float32) / degree[:, None]).astype(jnp.bfloat16)
    d_sum_tiles = d_sum.reshape(NODES // TILE, TILE, hidden)

    def backward_list(grad_tiles, inputs):
        list_id, tile_block, owners, sources, live_count = inputs
        dest_rows, src_rows, live_mask = placement(list_id, owners, sources, live_count)
        contrib = jnp.einsum("tij,tic->tjc", tile_block.astype(jnp.float32), d_sum_tiles[dest_rows].astype(jnp.float32), precision=lax.Precision.HIGHEST)
        return grad_tiles.at[src_rows].add(contrib * live_mask[:, None, None]), None

    grad_tiles, _ = lax.scan(backward_list, jnp.zeros((NODES // TILE, TILE, hidden), jnp.float32), (list_ids, flat_vals, flat_owner, flat_src, flat_count))
    d_feats = (jnp.dot(d_pre, w_self.T, preferred_element_type=jnp.float32) + grad_tiles.reshape(NODES, hidden)).astype(jnp.bfloat16)
    return (out_feats, d_feats, grad_self, grad_neigh)
```

```python
import functools

import jax
import jax.numpy as jnp
from jax import lax
from jax.experimental import pallas as pl
from jax.experimental.pallas import tpu as pltpu
from jax.sharding import PartitionSpec as P

F32 = jnp.float32
BF16 = jnp.bfloat16
MESH = pl.DeviceIdType.MESH
EXTRA = 16


def dot(x, y):
    return jnp.dot(x, y, preferred_element_type=F32)


def dot_nt(x, y):
    return lax.dot_general(x, y, (((1,), (1,)), ((), ())), preferred_element_type=F32)


def dot_tn(x, y):
    return lax.dot_general(x, y, (((0,), (0,)), ((), ())), preferred_element_type=F32)


def kernel(
    dims,
    feats_ref, w_self_ref, w_neigh_ref, tiles_ref, owner_ref, src_ref, count_ref, d_out_ref,
    out_ref, d_feats_ref, g_self_ref, g_neigh_ref,
    panel, dense, dense_sib, dense_t, x_send, x_recv, own, z_send, z_recv,
    gather, f_t, m_t, f_in, m_in, w_neigh_t, grad_acc, panel_acc, back_send, back_recv,
    gr_send, gr_recv,
    panel_s, panel_r, dense_s, dense_r, xs, xr, zs, zr, gzs, gzr, gxs, gxr, gcs, gcr,
    fs, fr, ms, mr, bs, br, grs, grr,
):
    R, A, B, T, hid, tiles, share, chunk, small = dims
    n_dom = A * B * 2
    rep = lax.axis_index("rep")
    dom = lax.axis_index("dom")
    c = lax.rem(dom, 2)
    b = lax.rem(lax.div(dom, 2), B)
    a = lax.div(dom, 2 * B)

    def dom_of(aa, bb, cc):
        return (aa * B + bb) * 2 + cc

    def plus(x, k, n):
        return lax.rem(x + k, n)

    sib = dom_of(a, b, 1 - c)

    def rcopy(src, dst, s, r, to_rep, to_dom):
        return pltpu.make_async_remote_copy(
            src_ref=src, dst_ref=dst, send_sem=s, recv_sem=r,
            device_id=(to_rep, to_dom), device_id_type=MESH,
        )

    barrier = pltpu.get_barrier_semaphore()
    for k in range(1, n_dom):
        pl.semaphore_signal(barrier, inc=1, device_id=(rep, plus(dom, k, n_dom)), device_id_type=MESH)
    for k in range(1, R):
        for cc in range(2):
            pl.semaphore_signal(
                barrier, inc=1, device_id=(plus(rep, k, R), dom_of(a, b, cc)), device_id_type=MESH
            )

    keys = None
    if small:
        keys = [
            jnp.where(t < count_ref[0], owner_ref[t] * R + src_ref[t], -1) for t in range(tiles)
        ]

    def place(pair):
        if small:
            at, live = jnp.int32(0), jnp.int32(0)
            for t in range(tiles):
                hit = keys[t] == pair
                at = jnp.where(hit, t, at)
                live = jnp.where(hit, 1, live)
            return at, live

        def look(t, state):
            hit = (owner_ref[t] * R + src_ref[t] == pair) & (t < count_ref[0])
            return jnp.where(hit, t, state[0]), jnp.where(hit, 1, state[1])

        return lax.fori_loop(0, tiles, look, (jnp.int32(0), jnp.int32(0)))

    def build(cc, bb):
        def one(aa, _):
            d = dom_of(aa, bb, cc)
            for s in range(R):
                at, live = place(d * R + s)
                mask = jnp.full((T, T), live.astype(F32), F32).astype(BF16)
                dense[cc, bb, aa, :, s * T:(s + 1) * T] = tiles_ref[at] * mask
            return 0
        if small:
            for aa in range(A):
                one(aa, 0)
        else:
            lax.fori_loop(0, A, one, 0)

    for kb in list(range(1, B)) + [0]:
        build(1 - c, plus(b, kb, B))

    f_t[...] = feats_ref[...].T
    panel[c, pl.ds(pl.multiple_of(rep * T, T), T), :] = feats_ref[...]

    pl.semaphore_wait(barrier, n_dom - 1 + 2 * (R - 1))

    copies = []
    panel_in = []
    for kr in range(R):
        for kc in range(2):
            if kr == 0 and kc == 0:
                continue
            to_c = plus(c, kc, 2)
            cp = rcopy(
                feats_ref, panel.at[c, pl.ds(pl.multiple_of(rep * T, T), T)],
                panel_s.at[kr * 2 + kc], panel_r.at[kr * 2 + kc], plus(rep, R - kr, R),
                dom_of(a, b, to_c),
            )
            cp.start()
            copies.append(cp)
            panel_in.append(cp)
    dense_in = {}
    for kb in list(range(1, B)) + [0]:
        bb = plus(b, kb, B)
        cp = rcopy(dense.at[1 - c, bb], dense_sib.at[bb], dense_s.at[kb], dense_r.at[kb], rep, sib)
        cp.start()
        copies.append(cp)
        dense_in[kb] = cp

    def scatter(src, dst, s, r):
        for k in range(1, n_dom):
            to = plus(dom, k, n_dom)
            row = pl.multiple_of(lax.div(to * share, chunk) * chunk, chunk)
            cp = rcopy(src.at[pl.ds(row, chunk)], dst.at[dom], s.at[k], r.at[k], rep, to)
            cp.start()
            copies.append(cp)
        row = pl.multiple_of(lax.div(dom * share, chunk) * chunk, chunk)
        dst[dom] = src[pl.ds(row, chunk), :]

    def scatter_wait(src, dst, s, r):
        for k in range(1, n_dom):
            frm = plus(dom, n_dom - k, n_dom)
            rcopy(src.at[pl.ds(0, chunk)], dst.at[frm], s.at[k], r.at[k], rep, frm).wait_recv()

    scatter(f_t, f_in, fs, fr)
    for kb in list(range(1, B)) + [0]:
        build(c, plus(b, kb, B))

    ones = jnp.ones((EXTRA, R * T), BF16)

    def block_sum(bb, aa):
        top = dot(dense[c, bb, aa], panel[c]) + dot(dense_sib[bb, aa], panel[1 - c])
        deg = dot_nt(ones, dense[c, bb, aa]) + dot_nt(ones, dense_sib[bb, aa])
        return top, deg

    def pack(dst, top, row):
        high = row.astype(BF16)
        dst[0:T, :] = top.astype(BF16)
        dst[T:T + EXTRA, 0:T] = high
        dst[T:T + EXTRA, T:2 * T] = (row - high.astype(F32)).astype(BF16)

    for cp in panel_in:
        cp.wait_recv()
    order = [2, 3, 1, 0] if A == 4 else list(range(1, A)) + [0]
    for kb in range(1, B):
        dense_in[kb].wait_recv()
        bb = plus(b, kb, B)
        for ka in order:
            aa = plus(a, ka, A)
            top, deg = block_sum(bb, aa)
            pack(x_send.at[kb - 1, ka], top, deg)
            i = (kb - 1) * A + ka
            cp = rcopy(x_send.at[kb - 1, ka], x_recv.at[kb - 1, ka], xs.at[i], xr.at[i], rep,
                       dom_of(a, bb, c))
            cp.start()
            copies.append(cp)
    dense_in[0].wait_recv()
    for ka in order:
        top, deg = block_sum(b, plus(a, ka, A))
        own[ka, 0:T, :] = top
        own[ka, T:T + EXTRA, 0:T] = deg

    w_neigh_t[...] = w_neigh_ref[...].T
    pre_self = dot(feats_ref[...], w_self_ref[...])
    if small:
        for aa in range(A):
            for bb in range(B):
                for cc in range(2):
                    dense_t[aa, bb, :, cc * T:(cc + 1) * T] = dense[cc, bb, aa].T

    def with_x(ka):
        top = own[ka, 0:T, :]
        deg = own[ka, T:T + EXTRA, 0:T]
        for kb in range(1, B):
            i = (kb - 1) * A + ka
            rcopy(x_send.at[kb - 1, ka], x_recv.at[kb - 1, ka], xs.at[i], xr.at[i], rep, sib).wait_recv()
            got = x_recv[kb - 1, ka].astype(F32)
            top = top + got[0:T]
            deg = deg + got[T:, 0:T] + got[T:, T:2 * T]
        return top, deg

    for ka in order[:-1]:
        top, deg = with_x(ka)
        pack(z_send.at[ka], top, deg)
        cp = rcopy(z_send.at[ka], z_recv.at[ka], zs.at[ka], zr.at[ka], rep,
                   dom_of(plus(a, ka, A), b, c))
        cp.start()
        copies.append(cp)
    top, deg = with_x(0)
    for ka in order[:-1]:
        rcopy(z_send.at[ka], z_recv.at[ka], zs.at[ka], zr.at[ka], rep, sib).wait_recv()
        got = z_recv[ka].astype(F32)
        top = top + got[0:T]
        deg = deg + got[T:, 0:T] + got[T:, T:2 * T]

    inv = 1.0 / (1.0 + deg)

    def as_column(row):
        col = jnp.broadcast_to(row[0:1, :], (T, T)).T
        return jnp.concatenate([col] * (hid // T), axis=1)

    mean = (top * as_column(inv)).astype(BF16)
    pre = pre_self + dot(mean, w_neigh_ref[...])
    g = jax.nn.sigmoid(pre)
    d_pre = (d_out_ref[...].astype(F32) * g * (1.0 + pre * (1.0 - g))).astype(BF16)
    mine = gather.at[a, b, c]
    pack(mine, d_pre, inv)

    def send_a(ka):
        cp = rcopy(mine, mine, gzs.at[ka], gzr.at[ka], rep, dom_of(plus(a, ka, A), b, c))
        cp.start()
        copies.append(cp)

    def block_at(ka, kb, cc):
        return gather.at[plus(a, A - ka, A), plus(b, B - kb, B), cc]

    def send_b(ka):
        blk = block_at(ka, 0, c)
        for kb in range(1, B):
            i = kb * A + ka
            cp = rcopy(blk, blk, gxs.at[i], gxr.at[i], rep, dom_of(a, plus(b, kb, B), c))
            cp.start()
            copies.append(cp)

    def send_c(ka, kb):
        blk = block_at(ka, kb, c)
        i = kb * A + ka
        cp = rcopy(blk, blk, gcs.at[i], gcr.at[i], rep, sib)
        cp.start()
        copies.append(cp)

    for ka in order[:-1]:
        send_a(ka)
    send_b(0)
    send_c(0, 0)
    out_ref[...] = (pre * g).astype(BF16)
    m_t[...] = mean.T
    scatter(m_t, m_in, ms, mr)
    d_self = dot_nt(d_pre, w_self_ref[...])

    panel_acc[...] = jnp.zeros_like(panel_acc)
    grad_acc[...] = jnp.zeros_like(grad_acc)

    def wait_c(ka, kb):
        blk = block_at(ka, kb, 1 - c)
        i = kb * A + ka
        rcopy(blk, blk, gcs.at[i], gcr.at[i], rep, sib).wait_recv()

    def use_pair(ka, kb):
        wait_c(ka, kb)
        aa, bb = plus(a, A - ka, A), plus(b, B - kb, B)
        d = [gather[aa, bb, cc, 0:T, :] for cc in range(2)]
        both = jnp.concatenate(d, axis=0)
        cols = []
        for cc in range(2):
            row = gather[aa, bb, cc, T:T + EXTRA, :].astype(F32)
            cols.append(as_column(row[:, 0:T] + row[:, T:2 * T]))
        d_sum = (dot(both, w_neigh_t[...]) * jnp.concatenate(cols, axis=0)).astype(BF16)
        if small:
            panel_acc[...] += dot(dense_t[aa, bb], d_sum)
        else:
            for cc in range(2):
                for s in range(R):
                    panel_acc[s * T:(s + 1) * T, :] += dot_tn(
                        dense[cc, bb, aa, :, s * T:(s + 1) * T], d_sum[cc * T:(cc + 1) * T]
                    )

    later = []
    for ka in [0] + order[:-1]:
        if ka > 0:
            blk = block_at(ka, 0, c)
            rcopy(blk, blk, gzs.at[ka], gzr.at[ka], rep, sib).wait_recv()
            send_b(ka)
            send_c(ka, 0)
        for kb in range(1, B):
            blk = block_at(ka, kb, c)
            i = kb * A + ka
            rcopy(blk, blk, gxs.at[i], gxr.at[i], rep, sib).wait_recv()
            send_c(ka, kb)
        for pair in later:
            use_pair(*pair)
        later = [(ka, kb) for kb in range(B)]
    for pair in later:
        use_pair(*pair)

    back = []
    for kr in range(1, R):
        to = plus(rep, kr, R)
        rows = pl.ds(pl.multiple_of(to * T, T), T)
        back_send[kr] = panel_acc[rows, :].astype(BF16)
        cp = rcopy(back_send.at[kr], back_recv.at[kr], bs.at[kr], br.at[kr], to, dom)
        cp.start()
        back.append(cp)

    scatter_wait(f_t, f_in, fs, fr)
    scatter_wait(m_t, m_in, ms, mr)

    def grad_pair(p, _):
        aa, bb = lax.div(p, B), lax.rem(p, B)
        lhs = []
        for ref in (f_in, m_in):
            lhs.append(jnp.concatenate([ref[2 * p], ref[2 * p + 1]], axis=1))
        rhs = jnp.concatenate([gather[aa, bb, cc, 0:T, :] for cc in range(2)], axis=0)
        grad_acc[...] += dot(jnp.concatenate(lhs, axis=0), rhs)
        return 0

    if small:
        for p in range(A * B):
            grad_pair(p, 0)
    else:
        lax.fori_loop(0, A * B, grad_pair, 0)
    gr_send[...] = grad_acc[...]
    for kr in range(1, R):
        cp = rcopy(gr_send, gr_recv.at[kr], grs.at[kr], grr.at[kr], plus(rep, kr, R), dom)
        cp.start()
        back.append(cp)

    mine_rows = pl.ds(pl.multiple_of(rep * T, T), T)
    total = d_self + panel_acc[mine_rows, :]
    for kr in range(1, R):
        back[kr - 1].wait_recv()
        total = total + back_recv[kr].astype(F32)
    d_feats_ref[...] = total.astype(BF16)
    grads = grad_acc[...]
    for kr in range(1, R):
        back[R - 1 + kr - 1].wait_recv()
        grads = grads + gr_recv[kr]
    at = lax.rem(dom * share, chunk)
    for i, ref in enumerate((g_self_ref, g_neigh_ref)):
        part = grads[i * chunk:(i + 1) * chunk]
        res = part[0:share]
        for k in range(1, chunk // share):
            res = jnp.where(at == k * share, part[k * share:(k + 1) * share], res)
        ref[...] = res

    for cp in copies + back:
        cp.wait_send()


def per_device(feats, w_self, w_neigh, tile_vals, tile_owner, tile_src, tile_count, d_out):
    R = lax.axis_size("rep")
    n_dom = lax.axis_size("dom")
    A = 4
    B = n_dom // (2 * A)
    T, hid = feats.shape
    tiles = tile_vals.shape[2]
    share = hid // n_dom
    chunk = max(share, 16)
    small = tiles <= 16
    msg = T + EXTRA
    dims = (R, A, B, T, hid, tiles, share, chunk, small)
    vmem = pl.BlockSpec(memory_space=pltpu.VMEM)
    smem = pl.BlockSpec(memory_space=pltpu.SMEM)
    dma = pltpu.SemaphoreType.DMA
    scratch = [
        pltpu.VMEM((2, R * T, hid), BF16),
        pltpu.VMEM((2, B, A, T, R * T), BF16),
        pltpu.VMEM((B, A, T, R * T), BF16),
        pltpu.VMEM((A, B, R * T, 2 * T) if small else (1, 1, 16, 128), BF16),
        pltpu.VMEM((B - 1, A, msg, hid), BF16),
        pltpu.VMEM((B - 1, A, msg, hid), BF16),
        pltpu.VMEM((A, msg, hid), F32),
        pltpu.VMEM((A, msg, hid), BF16),
        pltpu.VMEM((A, msg, hid), BF16),
        pltpu.VMEM((A, B, 2, msg, hid), BF16),
        pltpu.VMEM((hid, T), BF16),
        pltpu.VMEM((hid, T), BF16),
        pltpu.VMEM((n_dom, chunk, T), BF16),
        pltpu.VMEM((n_dom, chunk, T), BF16),
        pltpu.VMEM((hid, hid), BF16),
        pltpu.VMEM((2 * chunk, hid), F32),
        pltpu.VMEM((R * T, hid), F32),
        pltpu.VMEM((R, T, hid), BF16),
        pltpu.VMEM((R, T, hid), BF16),
        pltpu.VMEM((2 * chunk, hid), F32),
        pltpu.VMEM((R, 2 * chunk, hid), F32),
        dma((2 * R,)), dma((2 * R,)),
        dma((B,)), dma((B,)),
        dma(((B - 1) * A,)), dma(((B - 1) * A,)),
        dma((A,)), dma((A,)),
        dma((A,)), dma((A,)),
        dma((A * B,)), dma((A * B,)),
        dma((A * B,)), dma((A * B,)),
        dma((n_dom,)), dma((n_dom,)),
        dma((n_dom,)), dma((n_dom,)),
        dma((R,)), dma((R,)),
        dma((R,)), dma((R,)),
    ]
    return pl.pallas_call(
        functools.partial(kernel, dims),
        out_shape=(
            jax.ShapeDtypeStruct((T, hid), BF16),
            jax.ShapeDtypeStruct((T, hid), BF16),
            jax.ShapeDtypeStruct((share, hid), F32),
            jax.ShapeDtypeStruct((share, hid), F32),
        ),
        in_specs=[vmem, vmem, vmem, vmem, smem, smem, smem, vmem],
        out_specs=(vmem, vmem, vmem, vmem),
        scratch_shapes=scratch,
        compiler_params=pltpu.CompilerParams(
            collective_id=0, has_side_effects=True, vmem_limit_bytes=60 * 1024 * 1024
        ),
        name="sage_layer",
    )(
        feats, w_self, w_neigh, tile_vals[0, 0], tile_owner.reshape(-1), tile_src.reshape(-1),
        tile_count.reshape(-1), d_out,
    )


def solution(mesh):
    in_specs = (
        P(("rep", "dom"), None),
        P(),
        P(),
        P("rep", "dom", None, None, None),
        P("rep", "dom", None),
        P("rep", "dom", None),
        P("rep", "dom"),
        P(("rep", "dom"), None),
    )
    out_specs = (P(("rep", "dom"), None), P(("rep", "dom"), None), P("dom", None), P("dom", None))
    return jax.shard_map(
        per_device, mesh=mesh, in_specs=in_specs, out_specs=out_specs, check_vma=False
    )
```

```python
import functools

import jax
import jax.numpy as jnp
from jax import lax
from jax.experimental import pallas as pl
from jax.experimental.pallas import tpu as pltpu
from jax.sharding import PartitionSpec as P

F32 = jnp.float32
BF16 = jnp.bfloat16
MESH = pl.DeviceIdType.MESH
EXTRA = 16


def dot(x, y):
    return jnp.dot(x, y, preferred_element_type=F32)


def dot_nt(x, y):
    return lax.dot_general(x, y, (((1,), (1,)), ((), ())), preferred_element_type=F32)


def dot_tn(x, y):
    return lax.dot_general(x, y, (((0,), (0,)), ((), ())), preferred_element_type=F32)


def kernel(
    dims,
    feats_in, w_self_in, w_neigh_in, tiles_in, owner_in, src_in, count_in, d_out_in,
    out_ref, d_feats_ref, g_self_ref, g_neigh_ref,
    feats_ref, w_self_ref, w_neigh_ref, tiles_ref, owner_ref, src_ref, count_ref, d_out_ref, load_s,
    panel, dense, dense_sib, dense_t, x_send, x_recv, own, z_send, z_recv,
    gather, f_t, m_t, f_in, m_in, w_neigh_t, grad_acc, panel_acc, back_send, back_recv,
    gr_send, gr_recv,
    panel_s, panel_r, dense_s, dense_r, xs, xr, zs, zr, gzs, gzr, gxs, gxr, gcs, gcr,
    fs, fr, ms, mr, bs, br, grs, grr,
):
    R, A, B, T, hid, tiles, share, chunk, small = dims
    n_dom = A * B * 2
    rep = lax.axis_index("rep")
    dom = lax.axis_index("dom")
    c = lax.rem(dom, 2)
    b = lax.rem(lax.div(dom, 2), B)
    a = lax.div(dom, 2 * B)

    def dom_of(aa, bb, cc):
        return (aa * B + bb) * 2 + cc

    def plus(x, k, n):
        return lax.rem(x + k, n)

    sib = dom_of(a, b, 1 - c)

    def rcopy(src, dst, s, r, to_rep, to_dom):
        return pltpu.make_async_remote_copy(
            src_ref=src, dst_ref=dst, send_sem=s, recv_sem=r,
            device_id=(to_rep, to_dom), device_id_type=MESH,
        )

    barrier = pltpu.get_barrier_semaphore()
    for k in range(1, n_dom):
        pl.semaphore_signal(barrier, inc=1, device_id=(rep, plus(dom, k, n_dom)), device_id_type=MESH)
    for k in range(1, R):
        for cc in range(2):
            pl.semaphore_signal(
                barrier, inc=1, device_id=(plus(rep, k, R), dom_of(a, b, cc)), device_id_type=MESH
            )

    loads = []
    for i, (src, dst) in enumerate((
        (count_in, count_ref), (owner_in, owner_ref), (src_in, src_ref), (tiles_in, tiles_ref),
        (feats_in, feats_ref), (w_self_in, w_self_ref), (w_neigh_in, w_neigh_ref),
        (d_out_in, d_out_ref),
    )):
        cp = pltpu.make_async_copy(src, dst, load_s.at[i])
        cp.start()
        loads.append(cp)
    for cp in loads[:4]:
        cp.wait()

    keys = None
    if small:
        keys = [
            jnp.where(t < count_ref[0, 0], owner_ref[t] * R + src_ref[t], -1) for t in range(tiles)
        ]

    def place(pair):
        if small:
            at, live = jnp.int32(0), jnp.int32(0)
            for t in range(tiles):
                hit = keys[t] == pair
                at = jnp.where(hit, t, at)
                live = jnp.where(hit, 1, live)
            return at, live

        def look(t, state):
            hit = (owner_ref[t] * R + src_ref[t] == pair) & (t < count_ref[0, 0])
            return jnp.where(hit, t, state[0]), jnp.where(hit, 1, state[1])

        return lax.fori_loop(0, tiles, look, (jnp.int32(0), jnp.int32(0)))

    def build(cc, bb):
        def one(aa, _):
            d = dom_of(aa, bb, cc)
            for s in range(R):
                at, live = place(d * R + s)
                mask = jnp.full((T, T), live.astype(F32), F32).astype(BF16)
                dense[cc, bb, aa, :, s * T:(s + 1) * T] = tiles_ref[at] * mask
            return 0
        if small:
            for aa in range(A):
                one(aa, 0)
        else:
            lax.fori_loop(0, A, one, 0)

    for kb in list(range(1, B)) + [0]:
        build(1 - c, plus(b, kb, B))

    for cp in loads[4:]:
        cp.wait()
    f_t[...] = feats_ref[...].T
    panel[c, pl.ds(pl.multiple_of(rep * T, T), T), :] = feats_ref[...]

    pl.semaphore_wait(barrier, n_dom - 1 + 2 * (R - 1))

    copies = []
    panel_in = []
    for kr in range(R):
        for kc in range(2):
            if kr == 0 and kc == 0:
                continue
            to_c = plus(c, kc, 2)
            cp = rcopy(
                feats_ref, panel.at[c, pl.ds(pl.multiple_of(rep * T, T), T)],
                panel_s.at[kr * 2 + kc], panel_r.at[kr * 2 + kc], plus(rep, R - kr, R),
                dom_of(a, b, to_c),
            )
            cp.start()
            copies.append(cp)
            panel_in.append(cp)
    dense_in = {}
    for kb in list(range(1, B)) + [0]:
        bb = plus(b, kb, B)
        cp = rcopy(dense.at[1 - c, bb], dense_sib.at[bb], dense_s.at[kb], dense_r.at[kb], rep, sib)
        cp.start()
        copies.append(cp)
        dense_in[kb] = cp

    def scatter(src, dst, s, r):
        for k in range(1, n_dom):
            to = plus(dom, k, n_dom)
            row = pl.multiple_of(lax.div(to * share, chunk) * chunk, chunk)
            cp = rcopy(src.at[pl.ds(row, chunk)], dst.at[dom], s.at[k], r.at[k], rep, to)
            cp.start()
            copies.append(cp)
        row = pl.multiple_of(lax.div(dom * share, chunk) * chunk, chunk)
        dst[dom] = src[pl.ds(row, chunk), :]

    def scatter_wait(src, dst, s, r):
        for k in range(1, n_dom):
            frm = plus(dom, n_dom - k, n_dom)
            rcopy(src.at[pl.ds(0, chunk)], dst.at[frm], s.at[k], r.at[k], rep, frm).wait_recv()

    scatter(f_t, f_in, fs, fr)
    for kb in list(range(1, B)) + [0]:
        build(c, plus(b, kb, B))

    ones = jnp.ones((EXTRA, R * T), BF16)

    def block_sum(bb, aa):
        top = dot(dense[c, bb, aa], panel[c]) + dot(dense_sib[bb, aa], panel[1 - c])
        deg = dot_nt(ones, dense[c, bb, aa]) + dot_nt(ones, dense_sib[bb, aa])
        return top, deg

    def pack(dst, top, row):
        high = row.astype(BF16)
        dst[0:T, :] = top.astype(BF16)
        dst[T:T + EXTRA, 0:T] = high
        dst[T:T + EXTRA, T:2 * T] = (row - high.astype(F32)).astype(BF16)

    for cp in panel_in:
        cp.wait_recv()
    order = [2, 3, 1, 0] if A == 4 else list(range(1, A)) + [0]
    for kb in range(1, B):
        dense_in[kb].wait_recv()
        bb = plus(b, kb, B)
        for ka in order:
            aa = plus(a, ka, A)
            top, deg = block_sum(bb, aa)
            pack(x_send.at[kb - 1, ka], top, deg)
            i = (kb - 1) * A + ka
            cp = rcopy(x_send.at[kb - 1, ka], x_recv.at[kb - 1, ka], xs.at[i], xr.at[i], rep,
                       dom_of(a, bb, c))
            cp.start()
            copies.append(cp)
    dense_in[0].wait_recv()
    for ka in order:
        top, deg = block_sum(b, plus(a, ka, A))
        own[ka, 0:T, :] = top
        own[ka, T:T + EXTRA, 0:T] = deg

    def with_x(ka):
        top = own[ka, 0:T, :]
        deg = own[ka, T:T + EXTRA, 0:T]
        for kb in range(1, B):
            i = (kb - 1) * A + ka
            rcopy(x_send.at[kb - 1, ka], x_recv.at[kb - 1, ka], xs.at[i], xr.at[i], rep, sib).wait_recv()
            got = x_recv[kb - 1, ka].astype(F32)
            top = top + got[0:T]
            deg = deg + got[T:, 0:T] + got[T:, T:2 * T]
        return top, deg

    for ka in order[:-1]:
        top, deg = with_x(ka)
        pack(z_send.at[ka], top, deg)
        cp = rcopy(z_send.at[ka], z_recv.at[ka], zs.at[ka], zr.at[ka], rep,
                   dom_of(plus(a, ka, A), b, c))
        cp.start()
        copies.append(cp)
    w_neigh_t[...] = w_neigh_ref[...].T
    pre_self = dot(feats_ref[...], w_self_ref[...])
    if small:
        for aa in range(A):
            for bb in range(B):
                for cc in range(2):
                    dense_t[aa, bb, :, cc * T:(cc + 1) * T] = dense[cc, bb, aa].T

    top, deg = with_x(0)
    for ka in order[:-1]:
        rcopy(z_send.at[ka], z_recv.at[ka], zs.at[ka], zr.at[ka], rep, sib).wait_recv()
        got = z_recv[ka].astype(F32)
        top = top + got[0:T]
        deg = deg + got[T:, 0:T] + got[T:, T:2 * T]

    inv = 1.0 / (1.0 + deg)

    def as_column(row):
        col = jnp.broadcast_to(row[0:1, :], (T, T)).T
        return jnp.concatenate([col] * (hid // T), axis=1)

    mean = (top * as_column(inv)).astype(BF16)
    pre = pre_self + dot(mean, w_neigh_ref[...])
    g = jax.nn.sigmoid(pre)
    d_pre = (d_out_ref[...].astype(F32) * g * (1.0 + pre * (1.0 - g))).astype(BF16)
    mine = gather.at[a, b, c]
    pack(mine, d_pre, inv)

    def send_a(ka):
        cp = rcopy(mine, mine, gzs.at[ka], gzr.at[ka], rep, dom_of(plus(a, ka, A), b, c))
        cp.start()
        copies.append(cp)

    def block_at(ka, kb, cc):
        return gather.at[plus(a, A - ka, A), plus(b, B - kb, B), cc]

    def send_b(ka):
        blk = block_at(ka, 0, c)
        for kb in range(1, B):
            i = kb * A + ka
            cp = rcopy(blk, blk, gxs.at[i], gxr.at[i], rep, dom_of(a, plus(b, kb, B), c))
            cp.start()
            copies.append(cp)

    def send_c(ka, kb):
        blk = block_at(ka, kb, c)
        i = kb * A + ka
        cp = rcopy(blk, blk, gcs.at[i], gcr.at[i], rep, sib)
        cp.start()
        copies.append(cp)

    early = copies[:]
    copies.clear()
    for ka in order[:-1]:
        send_a(ka)
    send_b(0)
    send_c(0, 0)
    out_ref[...] = (pre * g).astype(BF16)
    m_t[...] = mean.T
    scatter(m_t, m_in, ms, mr)
    d_self = dot_nt(d_pre, w_self_ref[...])

    for cp in early:
        cp.wait_send()
    panel_acc[...] = jnp.zeros_like(panel_acc)
    grad_acc[...] = jnp.zeros_like(grad_acc)

    def wait_c(ka, kb):
        blk = block_at(ka, kb, 1 - c)
        i = kb * A + ka
        rcopy(blk, blk, gcs.at[i], gcr.at[i], rep, sib).wait_recv()

    def use_pair(ka, kb):
        wait_c(ka, kb)
        aa, bb = plus(a, A - ka, A), plus(b, B - kb, B)
        d = [gather[aa, bb, cc, 0:T, :] for cc in range(2)]
        both = jnp.concatenate(d, axis=0)
        cols = []
        for cc in range(2):
            row = gather[aa, bb, cc, T:T + EXTRA, :].astype(F32)
            cols.append(as_column(row[:, 0:T] + row[:, T:2 * T]))
        d_sum = (dot(both, w_neigh_t[...]) * jnp.concatenate(cols, axis=0)).astype(BF16)
        if small:
            panel_acc[...] += dot(dense_t[aa, bb], d_sum)
        else:
            for cc in range(2):
                for s in range(R):
                    panel_acc[s * T:(s + 1) * T, :] += dot_tn(
                        dense[cc, bb, aa, :, s * T:(s + 1) * T], d_sum[cc * T:(cc + 1) * T]
                    )

    def grads_of(ka, kb):
        aa, bb = plus(a, A - ka, A), plus(b, B - kb, B)
        first = dom_of(aa, bb, 0)
        lhs = [jnp.concatenate([r[first], r[first + 1]], axis=1) for r in (f_in, m_in)]
        rhs = jnp.concatenate([gather[aa, bb, cc, 0:T, :] for cc in range(2)], axis=0)
        grad_acc[...] += dot(jnp.concatenate(lhs, axis=0), rhs)

    done = []
    later = []
    for ka in [0] + order[:-1]:
        if ka > 0:
            blk = block_at(ka, 0, c)
            rcopy(blk, blk, gzs.at[ka], gzr.at[ka], rep, sib).wait_recv()
            send_b(ka)
            send_c(ka, 0)
        for kb in range(1, B):
            blk = block_at(ka, kb, c)
            i = kb * A + ka
            rcopy(blk, blk, gxs.at[i], gxr.at[i], rep, sib).wait_recv()
            send_c(ka, kb)
        for pair in later:
            use_pair(*pair)
        done += later
        later = [(ka, kb) for kb in range(B)]
    use_pair(*later[0])
    done.append(later.pop(0))
    scatter_wait(f_t, f_in, fs, fr)
    scatter_wait(m_t, m_in, ms, mr)
    for pair in done:
        grads_of(*pair)
    for pair in later:
        use_pair(*pair)

    back = []
    for kr in range(1, R):
        to = plus(rep, kr, R)
        rows = pl.ds(pl.multiple_of(to * T, T), T)
        back_send[kr] = panel_acc[rows, :].astype(BF16)
        cp = rcopy(back_send.at[kr], back_recv.at[kr], bs.at[kr], br.at[kr], to, dom)
        cp.start()
        back.append(cp)
    for pair in later:
        grads_of(*pair)
    gr_send[...] = grad_acc[...]
    for kr in range(1, R):
        cp = rcopy(gr_send, gr_recv.at[kr], grs.at[kr], grr.at[kr], plus(rep, kr, R), dom)
        cp.start()
        back.append(cp)
    for cp in copies:
        cp.wait_send()

    mine_rows = pl.ds(pl.multiple_of(rep * T, T), T)
    total = d_self + panel_acc[mine_rows, :]
    for kr in range(1, R):
        back[kr - 1].wait_recv()
        total = total + back_recv[kr].astype(F32)
    d_feats_ref[...] = total.astype(BF16)
    grads = grad_acc[...]
    for kr in range(1, R):
        back[R - 1 + kr - 1].wait_recv()
        grads = grads + gr_recv[kr]
    at = lax.rem(dom * share, chunk)
    for i, ref in enumerate((g_self_ref, g_neigh_ref)):
        part = grads[i * chunk:(i + 1) * chunk]
        res = part[0:share]
        for k in range(1, chunk // share):
            res = jnp.where(at == k * share, part[k * share:(k + 1) * share], res)
        ref[...] = res

    for cp in back:
        cp.wait_send()


def finish(*refs):
    n = (len(refs) - 1) // 2
    sems = refs[-1]
    moves = [pltpu.make_async_copy(refs[i], refs[n + i], sems.at[i]) for i in range(n)]
    for cp in moves:
        cp.start()
    for cp in moves:
        cp.wait()


def per_device(feats, w_self, w_neigh, tile_vals, tile_owner, tile_src, tile_count, d_out):
    R = lax.axis_size("rep")
    n_dom = lax.axis_size("dom")
    A = 4
    B = n_dom // (2 * A)
    T, hid = feats.shape
    tiles = tile_vals.shape[2]
    share = hid // n_dom
    chunk = max(share, 16)
    small = tiles <= 16
    msg = T + EXTRA
    dims = (R, A, B, T, hid, tiles, share, chunk, small)
    vmem = pl.BlockSpec(memory_space=pltpu.VMEM)
    anywhere = pl.BlockSpec(memory_space=pl.ANY)
    dma = pltpu.SemaphoreType.DMA
    scratch = [
        pltpu.VMEM((T, hid), BF16),
        pltpu.VMEM((hid, hid), BF16),
        pltpu.VMEM((hid, hid), BF16),
        pltpu.VMEM((tiles, T, T), BF16),
        pltpu.SMEM((tiles,), jnp.int32),
        pltpu.SMEM((tiles,), jnp.int32),
        pltpu.SMEM((1, 1), jnp.int32),
        pltpu.VMEM((T, hid), BF16),
        dma((8,)),
        pltpu.VMEM((2, R * T, hid), BF16),
        pltpu.VMEM((2, B, A, T, R * T), BF16),
        pltpu.VMEM((B, A, T, R * T), BF16),
        pltpu.VMEM((A, B, R * T, 2 * T) if small else (1, 1, 16, 128), BF16),
        pltpu.VMEM((B - 1, A, msg, hid), BF16),
        pltpu.VMEM((B - 1, A, msg, hid), BF16),
        pltpu.VMEM((A, msg, hid), F32),
        pltpu.VMEM((A, msg, hid), BF16),
        pltpu.VMEM((A, msg, hid), BF16),
        pltpu.VMEM((A, B, 2, msg, hid), BF16),
        pltpu.VMEM((hid, T), BF16),
        pltpu.VMEM((hid, T), BF16),
        pltpu.VMEM((n_dom, chunk, T), BF16),
        pltpu.VMEM((n_dom, chunk, T), BF16),
        pltpu.VMEM((hid, hid), BF16),
        pltpu.VMEM((2 * chunk, hid), F32),
        pltpu.VMEM((R * T, hid), F32),
        pltpu.VMEM((R, T, hid), BF16),
        pltpu.VMEM((R, T, hid), BF16),
        pltpu.VMEM((2 * chunk, hid), F32),
        pltpu.VMEM((R, 2 * chunk, hid), F32),
        dma((2 * R,)), dma((2 * R,)),
        dma((B,)), dma((B,)),
        dma(((B - 1) * A,)), dma(((B - 1) * A,)),
        dma((A,)), dma((A,)),
        dma((A,)), dma((A,)),
        dma((A * B,)), dma((A * B,)),
        dma((A * B,)), dma((A * B,)),
        dma((n_dom,)), dma((n_dom,)),
        dma((n_dom,)), dma((n_dom,)),
        dma((R,)), dma((R,)),
        dma((R,)), dma((R,)),
    ]
    results = pl.pallas_call(
        functools.partial(kernel, dims),
        out_shape=(
            pltpu.VMEM((T, hid), BF16),
            pltpu.VMEM((T, hid), BF16),
            pltpu.VMEM((share, hid), F32),
            pltpu.VMEM((share, hid), F32),
        ),
        in_specs=[anywhere] * 8,
        out_specs=(vmem, vmem, vmem, vmem),
        scratch_shapes=scratch,
        compiler_params=pltpu.CompilerParams(
            collective_id=0, has_side_effects=True, vmem_limit_bytes=60 * 1024 * 1024
        ),
        name="sage_layer",
    )(
        feats, w_self, w_neigh, tile_vals[0, 0], tile_owner.reshape(-1), tile_src.reshape(-1),
        tile_count, d_out,
    )
    return pl.pallas_call(
        finish,
        out_shape=tuple(jax.ShapeDtypeStruct(r.shape, r.dtype) for r in results),
        in_specs=[vmem] * 4,
        out_specs=(anywhere,) * 4,
        scratch_shapes=[dma((4,))],
        name="place_results",
    )(*results)


def solution(mesh):
    in_specs = (
        P(("rep", "dom"), None),
        P(),
        P(),
        P("rep", "dom", None, None, None),
        P("rep", "dom", None),
        P("rep", "dom", None),
        P("rep", "dom"),
        P(("rep", "dom"), None),
    )
    out_specs = (P(("rep", "dom"), None), P(("rep", "dom"), None), P("dom", None), P("dom", None))
    return jax.shard_map(
        per_device, mesh=mesh, in_specs=in_specs, out_specs=out_specs, check_vma=False
    )
```

```python
import functools

import jax
import jax.numpy as jnp
from jax import lax
from jax.experimental import pallas as pl
from jax.experimental.pallas import tpu as pltpu
from jax.sharding import PartitionSpec as P

F32 = jnp.float32
BF16 = jnp.bfloat16
MESH = pl.DeviceIdType.MESH
EXTRA = 16


def dot(x, y):
    return jnp.dot(x, y, preferred_element_type=F32)


def dot_nt(x, y):
    return lax.dot_general(x, y, (((1,), (1,)), ((), ())), preferred_element_type=F32)


def dot_tn(x, y):
    return lax.dot_general(x, y, (((0,), (0,)), ((), ())), preferred_element_type=F32)


def kernel(
    dims,
    feats_in, w_self_in, w_neigh_in, tiles_in, owner_in, src_in, count_in, d_out_in,
    out_ref, d_feats_ref, g_self_ref, g_neigh_ref,
    feats_ref, w_self_ref, w_neigh_ref, tiles_ref, owner_ref, src_ref, count_ref, d_out_ref, load_s,
    panel, dense, dense_sib, dense_t, x_send, x_recv, own, z_send, z_recv,
    gather, f_t, m_t, f_in, m_in, w_neigh_t, grad_acc, panel_acc, back_send, back_recv,
    gr_send, gr_recv,
    panel_s, panel_r, dense_s, dense_r, xs, xr, zs, zr, gzs, gzr, gxs, gxr, gcs, gcr,
    fs, fr, ms, mr, bs, br, grs, grr,
):
    R, A, B, T, hid, tiles, share, chunk, small = dims
    n_dom = A * B * 2
    rep = lax.axis_index("rep")
    dom = lax.axis_index("dom")
    c = lax.rem(dom, 2)
    b = lax.rem(lax.div(dom, 2), B)
    a = lax.div(dom, 2 * B)

    def dom_of(aa, bb, cc):
        return (aa * B + bb) * 2 + cc

    def plus(x, k, n):
        return lax.rem(x + k, n)

    sib = dom_of(a, b, 1 - c)

    def rcopy(src, dst, s, r, to_rep, to_dom):
        return pltpu.make_async_remote_copy(
            src_ref=src, dst_ref=dst, send_sem=s, recv_sem=r,
            device_id=(to_rep, to_dom), device_id_type=MESH,
        )

    barrier = pltpu.get_barrier_semaphore()
    for k in range(1, n_dom):
        pl.semaphore_signal(barrier, inc=1, device_id=(rep, plus(dom, k, n_dom)), device_id_type=MESH)
    for k in range(1, R):
        for cc in range(2):
            pl.semaphore_signal(
                barrier, inc=1, device_id=(plus(rep, k, R), dom_of(a, b, cc)), device_id_type=MESH
            )

    loads = []
    for i, (src, dst) in enumerate((
        (count_in, count_ref), (owner_in, owner_ref), (src_in, src_ref), (tiles_in, tiles_ref),
        (feats_in, feats_ref), (w_self_in, w_self_ref), (w_neigh_in, w_neigh_ref),
        (d_out_in, d_out_ref),
    )):
        cp = pltpu.make_async_copy(src, dst, load_s.at[i])
        cp.start()
        loads.append(cp)
    for cp in loads[:4]:
        cp.wait()

    keys = None
    if small:
        keys = [
            jnp.where(t < count_ref[0, 0], owner_ref[t] * R + src_ref[t], -1) for t in range(tiles)
        ]

    def place(pair):
        if small:
            at, live = jnp.int32(0), jnp.int32(0)
            for t in range(tiles):
                hit = keys[t] == pair
                at = jnp.where(hit, t, at)
                live = jnp.where(hit, 1, live)
            return at, live

        def look(t, state):
            hit = (owner_ref[t] * R + src_ref[t] == pair) & (t < count_ref[0, 0])
            return jnp.where(hit, t, state[0]), jnp.where(hit, 1, state[1])

        return lax.fori_loop(0, tiles, look, (jnp.int32(0), jnp.int32(0)))

    def build(cc, bb):
        def one(aa, _):
            d = dom_of(aa, bb, cc)
            for s in range(R):
                at, live = place(d * R + s)
                mask = jnp.full((T, T), live.astype(F32), F32).astype(BF16)
                dense[cc, bb, aa, :, s * T:(s + 1) * T] = tiles_ref[at] * mask
            return 0
        if small:
            for aa in range(A):
                one(aa, 0)
        else:
            lax.fori_loop(0, A, one, 0)

    for kb in list(range(1, B)) + [0]:
        build(1 - c, plus(b, kb, B))

    for cp in loads[4:]:
        cp.wait()
    f_t[...] = feats_ref[...].T
    panel[c, pl.ds(pl.multiple_of(rep * T, T), T), :] = feats_ref[...]

    pl.semaphore_wait(barrier, n_dom - 1 + 2 * (R - 1))

    copies = []
    panel_in = []
    for kr in range(R):
        for kc in range(2):
            if kr == 0 and kc == 0:
                continue
            to_c = plus(c, kc, 2)
            cp = rcopy(
                feats_ref, panel.at[c, pl.ds(pl.multiple_of(rep * T, T), T)],
                panel_s.at[kr * 2 + kc], panel_r.at[kr * 2 + kc], plus(rep, R - kr, R),
                dom_of(a, b, to_c),
            )
            cp.start()
            copies.append(cp)
            panel_in.append(cp)
    dense_in = {}
    for kb in list(range(1, B)) + [0]:
        bb = plus(b, kb, B)
        cp = rcopy(dense.at[1 - c, bb], dense_sib.at[bb], dense_s.at[kb], dense_r.at[kb], rep, sib)
        cp.start()
        copies.append(cp)
        dense_in[kb] = cp

    def scatter(src, dst, s, r):
        for k in range(1, n_dom):
            to = plus(dom, k, n_dom)
            row = pl.multiple_of(lax.div(to * share, chunk) * chunk, chunk)
            cp = rcopy(src.at[pl.ds(row, chunk)], dst.at[dom], s.at[k], r.at[k], rep, to)
            cp.start()
            copies.append(cp)
        row = pl.multiple_of(lax.div(dom * share, chunk) * chunk, chunk)
        dst[dom] = src[pl.ds(row, chunk), :]

    def scatter_wait(src, dst, s, r):
        for k in range(1, n_dom):
            frm = plus(dom, n_dom - k, n_dom)
            rcopy(src.at[pl.ds(0, chunk)], dst.at[frm], s.at[k], r.at[k], rep, frm).wait_recv()

    scatter(f_t, f_in, fs, fr)
    for kb in list(range(1, B)) + [0]:
        build(c, plus(b, kb, B))

    ones = jnp.ones((EXTRA, R * T), BF16)

    def block_sum(bb, aa):
        top = dot(dense[c, bb, aa], panel[c]) + dot(dense_sib[bb, aa], panel[1 - c])
        deg = dot_nt(ones, dense[c, bb, aa]) + dot_nt(ones, dense_sib[bb, aa])
        return top, deg

    def pack(dst, top, row):
        high = row.astype(BF16)
        dst[0:T, :] = top.astype(BF16)
        dst[T:T + EXTRA, 0:T] = high
        dst[T:T + EXTRA, T:2 * T] = (row - high.astype(F32)).astype(BF16)

    for cp in panel_in:
        cp.wait_recv()
    order = [2, 3, 1, 0] if A == 4 else list(range(1, A)) + [0]
    flying = []
    for kb in range(1, B):
        dense_in[kb].wait_recv()
        bb = plus(b, kb, B)
        for ka in order:
            aa = plus(a, ka, A)
            top, deg = block_sum(bb, aa)
            pack(x_send.at[kb - 1, ka], top, deg)
            i = (kb - 1) * A + ka
            if flying:
                flying.pop().wait_send()
            cp = rcopy(x_send.at[kb - 1, ka], x_recv.at[kb - 1, ka], xs.at[i], xr.at[i], rep,
                       dom_of(a, bb, c))
            cp.start()
            flying.append(cp)
    copies += flying
    dense_in[0].wait_recv()
    for ka in order:
        top, deg = block_sum(b, plus(a, ka, A))
        own[ka, 0:T, :] = top
        own[ka, T:T + EXTRA, 0:T] = deg

    def with_x(ka):
        top = own[ka, 0:T, :]
        deg = own[ka, T:T + EXTRA, 0:T]
        for kb in range(1, B):
            i = (kb - 1) * A + ka
            rcopy(x_send.at[kb - 1, ka], x_recv.at[kb - 1, ka], xs.at[i], xr.at[i], rep, sib).wait_recv()
            got = x_recv[kb - 1, ka].astype(F32)
            top = top + got[0:T]
            deg = deg + got[T:, 0:T] + got[T:, T:2 * T]
        return top, deg

    for ka in order[:-1]:
        top, deg = with_x(ka)
        pack(z_send.at[ka], top, deg)
        cp = rcopy(z_send.at[ka], z_recv.at[ka], zs.at[ka], zr.at[ka], rep,
                   dom_of(plus(a, ka, A), b, c))
        cp.start()
        copies.append(cp)
    w_neigh_t[...] = w_neigh_ref[...].T
    pre_self = dot(feats_ref[...], w_self_ref[...])
    if small:
        for aa in range(A):
            for bb in range(B):
                for cc in range(2):
                    dense_t[aa, bb, :, cc * T:(cc + 1) * T] = dense[cc, bb, aa].T

    top, deg = with_x(0)
    for ka in order[:-1]:
        rcopy(z_send.at[ka], z_recv.at[ka], zs.at[ka], zr.at[ka], rep, sib).wait_recv()
        got = z_recv[ka].astype(F32)
        top = top + got[0:T]
        deg = deg + got[T:, 0:T] + got[T:, T:2 * T]

    inv = 1.0 / (1.0 + deg)

    def as_column(row):
        col = jnp.broadcast_to(row[0:1, :], (T, T)).T
        return jnp.concatenate([col] * (hid // T), axis=1)

    mean = (top * as_column(inv)).astype(BF16)
    pre = pre_self + dot(mean, w_neigh_ref[...])
    g = jax.nn.sigmoid(pre)
    d_pre = (d_out_ref[...].astype(F32) * g * (1.0 + pre * (1.0 - g))).astype(BF16)
    mine = gather.at[a, b, c]
    pack(mine, d_pre, inv)

    def send_a(ka):
        cp = rcopy(mine, mine, gzs.at[ka], gzr.at[ka], rep, dom_of(plus(a, ka, A), b, c))
        cp.start()
        return cp

    def block_at(ka, kb, cc):
        return gather.at[plus(a, A - ka, A), plus(b, B - kb, B), cc]

    def send_b(ka):
        blk = block_at(ka, 0, c)
        for kb in range(1, B):
            i = kb * A + ka
            cp = rcopy(blk, blk, gxs.at[i], gxr.at[i], rep, dom_of(a, plus(b, kb, B), c))
            cp.start()
            copies.append(cp)

    def send_c(ka, kb):
        blk = block_at(ka, kb, c)
        i = kb * A + ka
        cp = rcopy(blk, blk, gcs.at[i], gcr.at[i], rep, sib)
        cp.start()
        copies.append(cp)

    early = copies[:]
    copies.clear()
    cp = send_a(order[0])
    send_b(0)
    send_c(0, 0)
    out_ref[...] = (pre * g).astype(BF16)
    m_t[...] = mean.T
    d_self = dot_nt(d_pre, w_self_ref[...])
    for ec in early:
        ec.wait_send()
    panel_acc[...] = jnp.zeros_like(panel_acc)
    grad_acc[...] = jnp.zeros_like(grad_acc)
    for ka in order[1:-1]:
        cp.wait_send()
        cp = send_a(ka)
    copies.append(cp)
    scatter(m_t, m_in, ms, mr)

    def wait_c(ka, kb):
        blk = block_at(ka, kb, 1 - c)
        i = kb * A + ka
        rcopy(blk, blk, gcs.at[i], gcr.at[i], rep, sib).wait_recv()

    def use_pair(ka, kb):
        wait_c(ka, kb)
        aa, bb = plus(a, A - ka, A), plus(b, B - kb, B)
        d = [gather[aa, bb, cc, 0:T, :] for cc in range(2)]
        both = jnp.concatenate(d, axis=0)
        cols = []
        for cc in range(2):
            row = gather[aa, bb, cc, T:T + EXTRA, :].astype(F32)
            cols.append(as_column(row[:, 0:T] + row[:, T:2 * T]))
        d_sum = (dot(both, w_neigh_t[...]) * jnp.concatenate(cols, axis=0)).astype(BF16)
        if small:
            panel_acc[...] += dot(dense_t[aa, bb], d_sum)
        else:
            for cc in range(2):
                for s in range(R):
                    panel_acc[s * T:(s + 1) * T, :] += dot_tn(
                        dense[cc, bb, aa, :, s * T:(s + 1) * T], d_sum[cc * T:(cc + 1) * T]
                    )

    def grads_of(ka, kb):
        aa, bb = plus(a, A - ka, A), plus(b, B - kb, B)
        first = dom_of(aa, bb, 0)
        lhs = [jnp.concatenate([r[first], r[first + 1]], axis=1) for r in (f_in, m_in)]
        rhs = jnp.concatenate([gather[aa, bb, cc, 0:T, :] for cc in range(2)], axis=0)
        grad_acc[...] += dot(jnp.concatenate(lhs, axis=0), rhs)

    done = []
    later = []
    for ka in [0] + order[:-1]:
        if ka > 0:
            blk = block_at(ka, 0, c)
            rcopy(blk, blk, gzs.at[ka], gzr.at[ka], rep, sib).wait_recv()
            send_b(ka)
            send_c(ka, 0)
        for kb in range(1, B):
            blk = block_at(ka, kb, c)
            i = kb * A + ka
            rcopy(blk, blk, gxs.at[i], gxr.at[i], rep, sib).wait_recv()
            send_c(ka, kb)
        for pair in later:
            use_pair(*pair)
        done += later
        later = [(ka, kb) for kb in range(B)]
    use_pair(*later[0])
    done.append(later.pop(0))
    scatter_wait(f_t, f_in, fs, fr)
    scatter_wait(m_t, m_in, ms, mr)
    for pair in done:
        grads_of(*pair)
    for pair in later:
        use_pair(*pair)

    back = []
    for kr in range(1, R):
        to = plus(rep, kr, R)
        rows = pl.ds(pl.multiple_of(to * T, T), T)
        back_send[kr] = panel_acc[rows, :].astype(BF16)
        cp = rcopy(back_send.at[kr], back_recv.at[kr], bs.at[kr], br.at[kr], to, dom)
        cp.start()
        back.append(cp)
    for pair in later:
        grads_of(*pair)
    gr_send[...] = grad_acc[...]
    for kr in range(1, R):
        cp = rcopy(gr_send, gr_recv.at[kr], grs.at[kr], grr.at[kr], plus(rep, kr, R), dom)
        cp.start()
        back.append(cp)
    for cp in copies:
        cp.wait_send()

    mine_rows = pl.ds(pl.multiple_of(rep * T, T), T)
    total = d_self + panel_acc[mine_rows, :]
    for kr in range(1, R):
        back[kr - 1].wait_recv()
        total = total + back_recv[kr].astype(F32)
    d_feats_ref[...] = total.astype(BF16)
    grads = grad_acc[...]
    for kr in range(1, R):
        back[R - 1 + kr - 1].wait_recv()
        grads = grads + gr_recv[kr]
    at = lax.rem(dom * share, chunk)
    for i, ref in enumerate((g_self_ref, g_neigh_ref)):
        part = grads[i * chunk:(i + 1) * chunk]
        res = part[0:share]
        for k in range(1, chunk // share):
            res = jnp.where(at == k * share, part[k * share:(k + 1) * share], res)
        ref[...] = res

    for cp in back:
        cp.wait_send()


def finish(*refs):
    n = (len(refs) - 1) // 2
    sems = refs[-1]
    moves = [pltpu.make_async_copy(refs[i], refs[n + i], sems.at[i]) for i in range(n)]
    for cp in moves:
        cp.start()
    for cp in moves:
        cp.wait()


def per_device(feats, w_self, w_neigh, tile_vals, tile_owner, tile_src, tile_count, d_out):
    R = lax.axis_size("rep")
    n_dom = lax.axis_size("dom")
    A = 4
    B = n_dom // (2 * A)
    T, hid = feats.shape
    tiles = tile_vals.shape[2]
    share = hid // n_dom
    chunk = max(share, 16)
    small = tiles <= 16
    msg = T + EXTRA
    dims = (R, A, B, T, hid, tiles, share, chunk, small)
    vmem = pl.BlockSpec(memory_space=pltpu.VMEM)
    anywhere = pl.BlockSpec(memory_space=pl.ANY)
    dma = pltpu.SemaphoreType.DMA
    scratch = [
        pltpu.VMEM((T, hid), BF16),
        pltpu.VMEM((hid, hid), BF16),
        pltpu.VMEM((hid, hid), BF16),
        pltpu.VMEM((tiles, T, T), BF16),
        pltpu.SMEM((tiles,), jnp.int32),
        pltpu.SMEM((tiles,), jnp.int32),
        pltpu.SMEM((1, 1), jnp.int32),
        pltpu.VMEM((T, hid), BF16),
        dma((8,)),
        pltpu.VMEM((2, R * T, hid), BF16),
        pltpu.VMEM((2, B, A, T, R * T), BF16),
        pltpu.VMEM((B, A, T, R * T), BF16),
        pltpu.VMEM((A, B, R * T, 2 * T) if small else (1, 1, 16, 128), BF16),
        pltpu.VMEM((B - 1, A, msg, hid), BF16),
        pltpu.VMEM((B - 1, A, msg, hid), BF16),
        pltpu.VMEM((A, msg, hid), F32),
        pltpu.VMEM((A, msg, hid), BF16),
        pltpu.VMEM((A, msg, hid), BF16),
        pltpu.VMEM((A, B, 2, msg, hid), BF16),
        pltpu.VMEM((hid, T), BF16),
        pltpu.VMEM((hid, T), BF16),
        pltpu.VMEM((n_dom, chunk, T), BF16),
        pltpu.VMEM((n_dom, chunk, T), BF16),
        pltpu.VMEM((hid, hid), BF16),
        pltpu.VMEM((2 * chunk, hid), F32),
        pltpu.VMEM((R * T, hid), F32),
        pltpu.VMEM((R, T, hid), BF16),
        pltpu.VMEM((R, T, hid), BF16),
        pltpu.VMEM((2 * chunk, hid), F32),
        pltpu.VMEM((R, 2 * chunk, hid), F32),
        dma((2 * R,)), dma((2 * R,)),
        dma((B,)), dma((B,)),
        dma(((B - 1) * A,)), dma(((B - 1) * A,)),
        dma((A,)), dma((A,)),
        dma((A,)), dma((A,)),
        dma((A * B,)), dma((A * B,)),
        dma((A * B,)), dma((A * B,)),
        dma((n_dom,)), dma((n_dom,)),
        dma((n_dom,)), dma((n_dom,)),
        dma((R,)), dma((R,)),
        dma((R,)), dma((R,)),
    ]
    results = pl.pallas_call(
        functools.partial(kernel, dims),
        out_shape=(
            pltpu.VMEM((T, hid), BF16),
            pltpu.VMEM((T, hid), BF16),
            pltpu.VMEM((share, hid), F32),
            pltpu.VMEM((share, hid), F32),
        ),
        in_specs=[anywhere] * 8,
        out_specs=(vmem, vmem, vmem, vmem),
        scratch_shapes=scratch,
        compiler_params=pltpu.CompilerParams(
            collective_id=0, has_side_effects=True, vmem_limit_bytes=60 * 1024 * 1024
        ),
        name="sage_layer",
    )(
        feats, w_self, w_neigh, tile_vals[0, 0], tile_owner.reshape(-1), tile_src.reshape(-1),
        tile_count, d_out,
    )
    return pl.pallas_call(
        finish,
        out_shape=tuple(jax.ShapeDtypeStruct(r.shape, r.dtype) for r in results),
        in_specs=[vmem] * 4,
        out_specs=(anywhere,) * 4,
        scratch_shapes=[dma((4,))],
        compiler_params=pltpu.CompilerParams(vmem_limit_bytes=1024 * 1024),
        name="place_results",
    )(*results)


def solution(mesh):
    in_specs = (
        P(("rep", "dom"), None),
        P(),
        P(),
        P("rep", "dom", None, None, None),
        P("rep", "dom", None),
        P("rep", "dom", None),
        P("rep", "dom"),
        P(("rep", "dom"), None),
    )
    out_specs = (P(("rep", "dom"), None), P(("rep", "dom"), None), P("dom", None), P("dom", None))
    return jax.shard_map(
        per_device, mesh=mesh, in_specs=in_specs, out_specs=out_specs, check_vma=False
    )
```

```python
import functools

import jax
import jax.numpy as jnp
from jax import lax
from jax.experimental import pallas as pl
from jax.experimental.pallas import tpu as pltpu
from jax.sharding import PartitionSpec as P

F32 = jnp.float32
BF16 = jnp.bfloat16
MESH = pl.DeviceIdType.MESH
CUT = 48
EXTRA = 16


def dot(x, y):
    return jnp.dot(x, y, preferred_element_type=F32)


def dot_nt(x, y):
    return lax.dot_general(x, y, (((1,), (1,)), ((), ())), preferred_element_type=F32)


def dot_tn(x, y):
    return lax.dot_general(x, y, (((0,), (0,)), ((), ())), preferred_element_type=F32)


def kernel(
    dims,
    feats_in, w_self_in, w_neigh_in, tiles_in, owner_in, src_in, count_in, d_out_in,
    out_ref, d_feats_ref, g_self_ref, g_neigh_ref,
    feats_ref, w_self_ref, w_neigh_ref, tiles_ref, owner_ref, src_ref, count_ref, d_out_ref, load_s,
    panel, dense, dense_sib, dense_t, x_send, x_recv, own, own2, z_send, z_recv, z2_send, z2_recv, x2_send, x2_recv,
    gather, f_t, m_t, f_in, m_in, w_neigh_t, grad_acc, panel_acc, back_send, back_recv,
    gr_send, gr_recv,
    panel_s, panel_r, dense_s, dense_r, xs, xr, zs, zr, z2s, z2r, x2s, x2r, gzs, gzr, gxs, gxr, gcs, gcr,
    fs, fr, ms, mr, bs, br, grs, grr,
):
    R, A, B, T, hid, tiles, share, chunk, small = dims
    n_dom = A * B * 2
    rep = lax.axis_index("rep")
    dom = lax.axis_index("dom")
    c = lax.rem(dom, 2)
    b = lax.rem(lax.div(dom, 2), B)
    a = lax.div(dom, 2 * B)

    def dom_of(aa, bb, cc):
        return (aa * B + bb) * 2 + cc

    def plus(x, k, n):
        return lax.rem(x + k, n)

    sib = dom_of(a, b, 1 - c)

    def rcopy(src, dst, s, r, to_rep, to_dom):
        return pltpu.make_async_remote_copy(
            src_ref=src, dst_ref=dst, send_sem=s, recv_sem=r,
            device_id=(to_rep, to_dom), device_id_type=MESH,
        )

    barrier = pltpu.get_barrier_semaphore()
    for k in range(1, n_dom):
        pl.semaphore_signal(barrier, inc=1, device_id=(rep, plus(dom, k, n_dom)), device_id_type=MESH)
    for k in range(1, R):
        for cc in range(2):
            pl.semaphore_signal(
                barrier, inc=1, device_id=(plus(rep, k, R), dom_of(a, b, cc)), device_id_type=MESH
            )

    loads = []
    for i, (src, dst) in enumerate((
        (count_in, count_ref), (owner_in, owner_ref), (src_in, src_ref), (tiles_in, tiles_ref),
        (feats_in, feats_ref), (w_self_in, w_self_ref), (w_neigh_in, w_neigh_ref),
        (d_out_in, d_out_ref),
    )):
        cp = pltpu.make_async_copy(src, dst, load_s.at[i])
        cp.start()
        loads.append(cp)
    for cp in loads[:4]:
        cp.wait()

    keys = None
    if small:
        keys = [
            jnp.where(t < count_ref[0, 0], owner_ref[t] * R + src_ref[t], -1) for t in range(tiles)
        ]

    def place(pair):
        if small:
            at, live = jnp.int32(0), jnp.int32(0)
            for t in range(tiles):
                hit = keys[t] == pair
                at = jnp.where(hit, t, at)
                live = jnp.where(hit, 1, live)
            return at, live

        def look(t, state):
            hit = (owner_ref[t] * R + src_ref[t] == pair) & (t < count_ref[0, 0])
            return jnp.where(hit, t, state[0]), jnp.where(hit, 1, state[1])

        return lax.fori_loop(0, tiles, look, (jnp.int32(0), jnp.int32(0)))

    def build(cc, bb):
        def one(aa, _):
            d = dom_of(aa, bb, cc)
            for s in range(R):
                at, live = place(d * R + s)
                mask = jnp.full((T, T), live.astype(F32), F32).astype(BF16)
                dense[cc, bb, aa, :, s * T:(s + 1) * T] = tiles_ref[at] * mask
            return 0
        if small:
            for aa in range(A):
                one(aa, 0)
        else:
            lax.fori_loop(0, A, one, 0)

    for kb in list(range(1, B)) + [0]:
        build(1 - c, plus(b, kb, B))

    for cp in loads[4:]:
        cp.wait()
    f_t[...] = feats_ref[...].T
    panel[c, pl.ds(pl.multiple_of(rep * T, T), T), :] = feats_ref[...]

    pl.semaphore_wait(barrier, n_dom - 1 + 2 * (R - 1))

    copies = []
    panel_in = []
    for kr in range(R):
        for kc in range(2):
            if kr == 0 and kc == 0:
                continue
            to_c = plus(c, kc, 2)
            cp = rcopy(
                feats_ref, panel.at[c, pl.ds(pl.multiple_of(rep * T, T), T)],
                panel_s.at[kr * 2 + kc], panel_r.at[kr * 2 + kc], plus(rep, R - kr, R),
                dom_of(a, b, to_c),
            )
            cp.start()
            copies.append(cp)
            panel_in.append(cp)
    dense_in = {}
    for kb in list(range(1, B)) + [0]:
        bb = plus(b, kb, B)
        cp = rcopy(dense.at[1 - c, bb], dense_sib.at[bb], dense_s.at[kb], dense_r.at[kb], rep, sib)
        cp.start()
        copies.append(cp)
        dense_in[kb] = cp

    def scatter(src, dst, s, r):
        for k in range(1, n_dom):
            to = plus(dom, k, n_dom)
            row = pl.multiple_of(lax.div(to * share, chunk) * chunk, chunk)
            cp = rcopy(src.at[pl.ds(row, chunk)], dst.at[dom], s.at[k], r.at[k], rep, to)
            cp.start()
            copies.append(cp)
        row = pl.multiple_of(lax.div(dom * share, chunk) * chunk, chunk)
        dst[dom] = src[pl.ds(row, chunk), :]

    def scatter_wait(src, dst, s, r):
        for k in range(1, n_dom):
            frm = plus(dom, n_dom - k, n_dom)
            rcopy(src.at[pl.ds(0, chunk)], dst.at[frm], s.at[k], r.at[k], rep, frm).wait_recv()

    scatter(f_t, f_in, fs, fr)
    for kb in list(range(1, B)) + [0]:
        build(c, plus(b, kb, B))

    ones = jnp.ones((EXTRA, R * T), BF16)

    def block_sum(bb, aa):
        top = dot(dense[c, bb, aa], panel[c]) + dot(dense_sib[bb, aa], panel[1 - c])
        deg = dot_nt(ones, dense[c, bb, aa]) + dot_nt(ones, dense_sib[bb, aa])
        return top, deg

    def pack(dst, top, row):
        n = top.shape[0]
        high = row.astype(BF16)
        dst[0:n, :] = top.astype(BF16)
        dst[n:n + EXTRA, 0:T] = high
        dst[n:n + EXTRA, T:2 * T] = (row - high.astype(F32)).astype(BF16)

    for cp in panel_in:
        cp.wait_recv()
    order = [2, 3, 1, 0] if A == 4 else list(range(1, A)) + [0]
    for kb in range(B):
        dense_in[kb].wait_recv()
    for ka in order:
        aa = plus(a, ka, A)
        for kb in list(range(1, B)) + [0]:
            bb = plus(b, kb, B)
            top, deg = block_sum(bb, aa)
            if ka > 0:
                z2_send[ka, kb * CUT:(kb + 1) * CUT, :] = top[0:CUT].astype(BF16)
            else:
                own2[kb] = top[0:CUT]
            if kb > 0:
                pack(x_send.at[kb - 1, ka], top[CUT:], deg)
                i = (kb - 1) * A + ka
                cp = rcopy(x_send.at[kb - 1, ka], x_recv.at[kb - 1, ka], xs.at[i], xr.at[i], rep,
                           dom_of(a, bb, c))
                cp.start()
                copies.append(cp)
            else:
                own[ka, 0:T - CUT, :] = top[CUT:]
                own[ka, T - CUT:T - CUT + EXTRA, 0:T] = deg
        if ka > 0:
            cp = rcopy(z2_send.at[ka], z2_recv.at[ka], z2s.at[ka], z2r.at[ka], rep, dom_of(aa, b, c))
            cp.start()
            copies.append(cp)

    low = T - CUT

    def with_x(ka):
        top = own[ka, 0:low, :]
        deg = own[ka, low:low + EXTRA, 0:T]
        for kb in range(1, B):
            i = (kb - 1) * A + ka
            rcopy(x_send.at[kb - 1, ka], x_recv.at[kb - 1, ka], xs.at[i], xr.at[i], rep, sib).wait_recv()
            got = x_recv[kb - 1, ka].astype(F32)
            top = top + got[0:low]
            deg = deg + got[low:, 0:T] + got[low:, T:2 * T]
        return top, deg

    for ka in order[:-1]:
        top, deg = with_x(ka)
        pack(z_send.at[ka], top, deg)
        cp = rcopy(z_send.at[ka], z_recv.at[ka], zs.at[ka], zr.at[ka], rep,
                   dom_of(plus(a, ka, A), b, c))
        cp.start()
        copies.append(cp)
    for ka in order[:-1]:
        rcopy(z2_send.at[ka], z2_recv.at[ka], z2s.at[ka], z2r.at[ka], rep, sib).wait_recv()
    for kb in list(range(1, B)) + [0]:
        part = own2[kb]
        for ka in range(1, A):
            part = part + z2_recv[ka, kb * CUT:(kb + 1) * CUT, :].astype(F32)
        if kb > 0:
            x2_send[kb] = part.astype(BF16)
            cp = rcopy(x2_send.at[kb], x2_recv.at[kb], x2s.at[kb], x2r.at[kb], rep,
                       dom_of(a, plus(b, kb, B), c))
            cp.start()
            copies.append(cp)
    head = part

    w_neigh_t[...] = w_neigh_ref[...].T
    pre_self = dot(feats_ref[...], w_self_ref[...])
    if small:
        for aa in range(A):
            for bb in range(B):
                for cc in range(2):
                    dense_t[aa, bb, :, cc * T:(cc + 1) * T] = dense[cc, bb, aa].T

    top, deg = with_x(0)
    for ka in order[:-1]:
        rcopy(z_send.at[ka], z_recv.at[ka], zs.at[ka], zr.at[ka], rep, sib).wait_recv()
        got = z_recv[ka].astype(F32)
        top = top + got[0:low]
        deg = deg + got[low:, 0:T] + got[low:, T:2 * T]
    for kb in range(1, B):
        rcopy(x2_send.at[kb], x2_recv.at[kb], x2s.at[kb], x2r.at[kb], rep, sib).wait_recv()
        head = head + x2_recv[kb].astype(F32)
    top = jnp.concatenate([head, top], axis=0)

    inv = 1.0 / (1.0 + deg)

    def as_column(row):
        col = jnp.broadcast_to(row[0:1, :], (T, T)).T
        return jnp.concatenate([col] * (hid // T), axis=1)

    mean = (top * as_column(inv)).astype(BF16)
    pre = pre_self + dot(mean, w_neigh_ref[...])
    g = jax.nn.sigmoid(pre)
    d_pre = (d_out_ref[...].astype(F32) * g * (1.0 + pre * (1.0 - g))).astype(BF16)
    mine = gather.at[a, b, c]
    pack(mine, d_pre, inv)

    def send_a(ka):
        cp = rcopy(mine, mine, gzs.at[ka], gzr.at[ka], rep, dom_of(plus(a, ka, A), b, c))
        cp.start()
        copies.append(cp)

    def block_at(ka, kb, cc):
        return gather.at[plus(a, A - ka, A), plus(b, B - kb, B), cc]

    def send_b(ka):
        blk = block_at(ka, 0, c)
        for kb in range(1, B):
            i = kb * A + ka
            cp = rcopy(blk, blk, gxs.at[i], gxr.at[i], rep, dom_of(a, plus(b, kb, B), c))
            cp.start()
            copies.append(cp)

    def send_c(ka, kb):
        blk = block_at(ka, kb, c)
        i = kb * A + ka
        cp = rcopy(blk, blk, gcs.at[i], gcr.at[i], rep, sib)
        cp.start()
        copies.append(cp)

    early = copies[:]
    copies.clear()
    for ka in order[:-1]:
        send_a(ka)
    send_b(0)
    send_c(0, 0)
    out_ref[...] = (pre * g).astype(BF16)
    m_t[...] = mean.T
    d_self = dot_nt(d_pre, w_self_ref[...])
    for ec in early:
        ec.wait_send()
    panel_acc[...] = jnp.zeros_like(panel_acc)
    grad_acc[...] = jnp.zeros_like(grad_acc)
    scatter(m_t, m_in, ms, mr)

    def wait_c(ka, kb):
        blk = block_at(ka, kb, 1 - c)
        i = kb * A + ka
        rcopy(blk, blk, gcs.at[i], gcr.at[i], rep, sib).wait_recv()

    def use_pair(ka, kb):
        wait_c(ka, kb)
        aa, bb = plus(a, A - ka, A), plus(b, B - kb, B)
        d = [gather[aa, bb, cc, 0:T, :] for cc in range(2)]
        both = jnp.concatenate(d, axis=0)
        cols = []
        for cc in range(2):
            row = gather[aa, bb, cc, T:T + EXTRA, :].astype(F32)
            cols.append(as_column(row[:, 0:T] + row[:, T:2 * T]))
        d_sum = (dot(both, w_neigh_t[...]) * jnp.concatenate(cols, axis=0)).astype(BF16)
        if small:
            panel_acc[...] += dot(dense_t[aa, bb], d_sum)
        else:
            for cc in range(2):
                for s in range(R):
                    panel_acc[s * T:(s + 1) * T, :] += dot_tn(
                        dense[cc, bb, aa, :, s * T:(s + 1) * T], d_sum[cc * T:(cc + 1) * T]
                    )

    def grads_of(ka, kb):
        aa, bb = plus(a, A - ka, A), plus(b, B - kb, B)
        first = dom_of(aa, bb, 0)
        lhs = [jnp.concatenate([r[first], r[first + 1]], axis=1) for r in (f_in, m_in)]
        rhs = jnp.concatenate([gather[aa, bb, cc, 0:T, :] for cc in range(2)], axis=0)
        grad_acc[...] += dot(jnp.concatenate(lhs, axis=0), rhs)

    done = []
    later = []
    for ka in [0] + order[:-1]:
        if ka > 0:
            blk = block_at(ka, 0, c)
            rcopy(blk, blk, gzs.at[ka], gzr.at[ka], rep, sib).wait_recv()
            send_b(ka)
            send_c(ka, 0)
        for kb in range(1, B):
            blk = block_at(ka, kb, c)
            i = kb * A + ka
            rcopy(blk, blk, gxs.at[i], gxr.at[i], rep, sib).wait_recv()
            send_c(ka, kb)
        for pair in later:
            use_pair(*pair)
        done += later
        later = [(ka, kb) for kb in range(B)]
    use_pair(*later[0])
    done.append(later.pop(0))
    scatter_wait(f_t, f_in, fs, fr)
    scatter_wait(m_t, m_in, ms, mr)
    for pair in done:
        grads_of(*pair)
    for pair in later:
        use_pair(*pair)

    back = []
    for kr in range(1, R):
        to = plus(rep, kr, R)
        rows = pl.ds(pl.multiple_of(to * T, T), T)
        back_send[kr] = panel_acc[rows, :].astype(BF16)
        cp = rcopy(back_send.at[kr], back_recv.at[kr], bs.at[kr], br.at[kr], to, dom)
        cp.start()
        back.append(cp)
    for pair in later:
        grads_of(*pair)
    gr_send[...] = grad_acc[...]
    for kr in range(1, R):
        cp = rcopy(gr_send, gr_recv.at[kr], grs.at[kr], grr.at[kr], plus(rep, kr, R), dom)
        cp.start()
        back.append(cp)
    for cp in copies:
        cp.wait_send()

    mine_rows = pl.ds(pl.multiple_of(rep * T, T), T)
    total = d_self + panel_acc[mine_rows, :]
    for kr in range(1, R):
        back[kr - 1].wait_recv()
        total = total + back_recv[kr].astype(F32)
    d_feats_ref[...] = total.astype(BF16)
    grads = grad_acc[...]
    for kr in range(1, R):
        back[R - 1 + kr - 1].wait_recv()
        grads = grads + gr_recv[kr]
    at = lax.rem(dom * share, chunk)
    for i, ref in enumerate((g_self_ref, g_neigh_ref)):
        part = grads[i * chunk:(i + 1) * chunk]
        res = part[0:share]
        for k in range(1, chunk // share):
            res = jnp.where(at == k * share, part[k * share:(k + 1) * share], res)
        ref[...] = res

    for cp in back:
        cp.wait_send()


def finish(*refs):
    n = (len(refs) - 1) // 2
    sems = refs[-1]
    moves = [pltpu.make_async_copy(refs[i], refs[n + i], sems.at[i]) for i in range(n)]
    for cp in moves:
        cp.start()
    for cp in moves:
        cp.wait()


def per_device(feats, w_self, w_neigh, tile_vals, tile_owner, tile_src, tile_count, d_out):
    R = lax.axis_size("rep")
    n_dom = lax.axis_size("dom")
    A = 4
    B = n_dom // (2 * A)
    T, hid = feats.shape
    tiles = tile_vals.shape[2]
    share = hid // n_dom
    chunk = max(share, 16)
    small = tiles <= 16
    msg = T + EXTRA
    dims = (R, A, B, T, hid, tiles, share, chunk, small)
    vmem = pl.BlockSpec(memory_space=pltpu.VMEM)
    anywhere = pl.BlockSpec(memory_space=pl.ANY)
    dma = pltpu.SemaphoreType.DMA
    scratch = [
        pltpu.VMEM((T, hid), BF16),
        pltpu.VMEM((hid, hid), BF16),
        pltpu.VMEM((hid, hid), BF16),
        pltpu.VMEM((tiles, T, T), BF16),
        pltpu.SMEM((tiles,), jnp.int32),
        pltpu.SMEM((tiles,), jnp.int32),
        pltpu.SMEM((1, 1), jnp.int32),
        pltpu.VMEM((T, hid), BF16),
        dma((8,)),
        pltpu.VMEM((2, R * T, hid), BF16),
        pltpu.VMEM((2, B, A, T, R * T), BF16),
        pltpu.VMEM((B, A, T, R * T), BF16),
        pltpu.VMEM((A, B, R * T, 2 * T) if small else (1, 1, 16, 128), BF16),
        pltpu.VMEM((B - 1, A, msg - CUT, hid), BF16),
        pltpu.VMEM((B - 1, A, msg - CUT, hid), BF16),
        pltpu.VMEM((A, msg - CUT, hid), F32),
        pltpu.VMEM((B, CUT, hid), F32),
        pltpu.VMEM((A, msg - CUT, hid), BF16),
        pltpu.VMEM((A, msg - CUT, hid), BF16),
        pltpu.VMEM((A, B * CUT, hid), BF16),
        pltpu.VMEM((A, B * CUT, hid), BF16),
        pltpu.VMEM((B, CUT, hid), BF16),
        pltpu.VMEM((B, CUT, hid), BF16),
        pltpu.VMEM((A, B, 2, msg, hid), BF16),
        pltpu.VMEM((hid, T), BF16),
        pltpu.VMEM((hid, T), BF16),
        pltpu.VMEM((n_dom, chunk, T), BF16),
        pltpu.VMEM((n_dom, chunk, T), BF16),
        pltpu.VMEM((hid, hid), BF16),
        pltpu.VMEM((2 * chunk, hid), F32),
        pltpu.VMEM((R * T, hid), F32),
        pltpu.VMEM((R, T, hid), BF16),
        pltpu.VMEM((R, T, hid), BF16),
        pltpu.VMEM((2 * chunk, hid), F32),
        pltpu.VMEM((R, 2 * chunk, hid), F32),
        dma((2 * R,)), dma((2 * R,)),
        dma((B,)), dma((B,)),
        dma(((B - 1) * A,)), dma(((B - 1) * A,)),
        dma((A,)), dma((A,)),
        dma((A,)), dma((A,)),
        dma((B,)), dma((B,)),
        dma((A,)), dma((A,)),
        dma((A * B,)), dma((A * B,)),
        dma((A * B,)), dma((A * B,)),
        dma((n_dom,)), dma((n_dom,)),
        dma((n_dom,)), dma((n_dom,)),
        dma((R,)), dma((R,)),
        dma((R,)), dma((R,)),
    ]
    results = pl.pallas_call(
        functools.partial(kernel, dims),
        out_shape=(
            pltpu.VMEM((T, hid), BF16),
            pltpu.VMEM((T, hid), BF16),
            pltpu.VMEM((share, hid), F32),
            pltpu.VMEM((share, hid), F32),
        ),
        in_specs=[anywhere] * 8,
        out_specs=(vmem, vmem, vmem, vmem),
        scratch_shapes=scratch,
        compiler_params=pltpu.CompilerParams(
            collective_id=0, has_side_effects=True, vmem_limit_bytes=60 * 1024 * 1024
        ),
        name="sage_layer",
    )(
        feats, w_self, w_neigh, tile_vals[0, 0], tile_owner.reshape(-1), tile_src.reshape(-1),
        tile_count, d_out,
    )
    return pl.pallas_call(
        finish,
        out_shape=tuple(jax.ShapeDtypeStruct(r.shape, r.dtype) for r in results),
        in_specs=[vmem] * 4,
        out_specs=(anywhere,) * 4,
        scratch_shapes=[dma((4,))],
        compiler_params=pltpu.CompilerParams(vmem_limit_bytes=1024 * 1024),
        name="place_results",
    )(*results)


def solution(mesh):
    in_specs = (
        P(("rep", "dom"), None),
        P(),
        P(),
        P("rep", "dom", None, None, None),
        P("rep", "dom", None),
        P("rep", "dom", None),
        P("rep", "dom"),
        P(("rep", "dom"), None),
    )
    out_specs = (P(("rep", "dom"), None), P(("rep", "dom"), None), P("dom", None), P("dom", None))
    return jax.shard_map(
        per_device, mesh=mesh, in_specs=in_specs, out_specs=out_specs, check_vma=False
    )
```

```python
import functools

import jax
import jax.numpy as jnp
from jax import lax
from jax.experimental import pallas as pl
from jax.experimental.pallas import tpu as pltpu
from jax.sharding import PartitionSpec as P

F32 = jnp.float32
BF16 = jnp.bfloat16
MESH = pl.DeviceIdType.MESH
CUT = 48
EXTRA = 16


def dot(x, y):
    return jnp.dot(x, y, preferred_element_type=F32)


def dot_nt(x, y):
    return lax.dot_general(x, y, (((1,), (1,)), ((), ())), preferred_element_type=F32)


def dot_tn(x, y):
    return lax.dot_general(x, y, (((0,), (0,)), ((), ())), preferred_element_type=F32)


def kernel(
    dims,
    feats_in, w_self_in, w_neigh_in, tiles_in, owner_in, src_in, count_in, d_out_in,
    out_ref, d_feats_ref, g_self_ref, g_neigh_ref,
    feats_ref, w_self_ref, w_neigh_ref, tiles_ref, owner_ref, src_ref, count_ref, d_out_ref, load_s,
    panel, dense, dense_sib, dense_t, x_send, x_recv, sums_by, z_send, z_recv, z2_send, z2_recv, x2_send, x2_recv,
    gather, f_t, m_t, row_sums, f_send, f_in, m_in, w_neigh_t, grad_acc, panel_acc, back_send, back_recv,
    gr_send, gr_recv,
    panel_s, panel_r, dense_s, dense_r, xs, xr, zs, zr, z2s, z2r, x2s, x2r, gzs, gzr, gxs, gxr, gcs, gcr,
    fs, fr, ms, mr, bs, br, grs, grr,
):
    R, A, B, T, hid, tiles, share, chunk, small = dims
    n_dom = A * B * 2
    rep = lax.axis_index("rep")
    dom = lax.axis_index("dom")
    c = lax.rem(dom, 2)
    b = lax.rem(lax.div(dom, 2), B)
    a = lax.div(dom, 2 * B)

    def dom_of(aa, bb, cc):
        return (aa * B + bb) * 2 + cc

    def plus(x, k, n):
        return lax.rem(x + k, n)

    sib = dom_of(a, b, 1 - c)

    def rcopy(src, dst, s, r, to_rep, to_dom):
        return pltpu.make_async_remote_copy(
            src_ref=src, dst_ref=dst, send_sem=s, recv_sem=r,
            device_id=(to_rep, to_dom), device_id_type=MESH,
        )

    barrier = pltpu.get_barrier_semaphore()
    for k in range(1, n_dom):
        pl.semaphore_signal(barrier, inc=1, device_id=(rep, plus(dom, k, n_dom)), device_id_type=MESH)
    for k in range(1, R):
        for cc in range(2):
            pl.semaphore_signal(
                barrier, inc=1, device_id=(plus(rep, k, R), dom_of(a, b, cc)), device_id_type=MESH
            )

    loads = []
    for i, (src, dst) in enumerate((
        (count_in, count_ref), (owner_in, owner_ref), (src_in, src_ref), (tiles_in, tiles_ref),
        (feats_in, feats_ref), (w_self_in, w_self_ref), (w_neigh_in, w_neigh_ref),
        (d_out_in, d_out_ref),
    )):
        cp = pltpu.make_async_copy(src, dst, load_s.at[i])
        cp.start()
        loads.append(cp)
    for cp in loads[:4]:
        cp.wait()

    keys = None
    if small:
        keys = [
            jnp.where(t < count_ref[0, 0], owner_ref[t] * R + src_ref[t], -1) for t in range(tiles)
        ]

    def place(pair):
        if small:
            at, live = jnp.int32(0), jnp.int32(0)
            for t in range(tiles):
                hit = keys[t] == pair
                at = jnp.where(hit, t, at)
                live = jnp.where(hit, 1, live)
            return at, live

        def look(t, state):
            hit = (owner_ref[t] * R + src_ref[t] == pair) & (t < count_ref[0, 0])
            return jnp.where(hit, t, state[0]), jnp.where(hit, 1, state[1])

        return lax.fori_loop(0, tiles, look, (jnp.int32(0), jnp.int32(0)))

    if small:
        sums = dot_nt(jnp.ones((EXTRA, T), BF16), tiles_ref[...].reshape(tiles * T, T))
        for t in range(tiles):
            row_sums[t] = sums[0:8, t * T:(t + 1) * T]
    else:
        def sum_tile(t, _):
            row_sums[t] = dot_nt(jnp.ones((EXTRA, T), BF16), tiles_ref[t])[0:8]
            return 0
        lax.fori_loop(0, tiles, sum_tile, 0)

    def build(cc, bb):
        def one(aa, _):
            d = dom_of(aa, bb, cc)
            for s in range(R):
                at, live = place(d * R + s)
                mask = jnp.full((T, T), live.astype(F32), F32).astype(BF16)
                dense[cc, bb, aa, :, s * T:(s + 1) * T] = tiles_ref[at] * mask
                part = row_sums[at] * live.astype(F32)
                deg = part if s == 0 else deg + part
            high = deg.astype(BF16).astype(F32)
            f_send[d, chunk:chunk + EXTRA, :] = jnp.concatenate([high, deg - high], axis=0).astype(BF16)
            return 0
        if small:
            for aa in range(A):
                one(aa, 0)
        else:
            lax.fori_loop(0, A, one, 0)

    for kb in list(range(1, B)) + [0]:
        build(1 - c, plus(b, kb, B))

    for cp in loads[4:]:
        cp.wait()
    f_t[...] = feats_ref[...].T
    for d in range(n_dom):
        row = d * share // chunk * chunk
        f_send[d, 0:chunk, :] = f_t[row:row + chunk, :]
    panel[c, pl.ds(pl.multiple_of(rep * T, T), T), :] = feats_ref[...]

    pl.semaphore_wait(barrier, n_dom - 1 + 2 * (R - 1))

    copies = []
    panel_in = []
    for kr in range(R):
        for kc in range(2):
            if kr == 0 and kc == 0:
                continue
            to_c = plus(c, kc, 2)
            cp = rcopy(
                feats_ref, panel.at[c, pl.ds(pl.multiple_of(rep * T, T), T)],
                panel_s.at[kr * 2 + kc], panel_r.at[kr * 2 + kc], plus(rep, R - kr, R),
                dom_of(a, b, to_c),
            )
            cp.start()
            copies.append(cp)
            panel_in.append(cp)
    dense_in = {}
    for kb in list(range(1, B)) + [0]:
        bb = plus(b, kb, B)
        cp = rcopy(dense.at[1 - c, bb], dense_sib.at[bb], dense_s.at[kb], dense_r.at[kb], rep, sib)
        cp.start()
        copies.append(cp)
        dense_in[kb] = cp

    def chunk_at(d):
        return pl.ds(pl.multiple_of(lax.div(d * share, chunk) * chunk, chunk), chunk)

    def scatter(pick, dst, s, r):
        for k in range(1, n_dom):
            to = plus(dom, k, n_dom)
            cp = rcopy(pick(to), dst.at[dom], s.at[k], r.at[k], rep, to)
            cp.start()
            copies.append(cp)

    def scatter_wait(pick, dst, s, r):
        for k in range(1, n_dom):
            frm = plus(dom, n_dom - k, n_dom)
            rcopy(pick(frm), dst.at[frm], s.at[k], r.at[k], rep, frm).wait_recv()

    def pick_f(d):
        return f_send.at[d]

    def pick_m(d):
        return m_t.at[chunk_at(d)]

    for kb in list(range(1, B)) + [0]:
        build(c, plus(b, kb, B))
    scatter(pick_f, f_in, fs, fr)
    f_in[dom] = f_send[dom]

    w_neigh_t[...] = w_neigh_ref[...].T
    pre_self = dot(feats_ref[...], w_self_ref[...])
    if small:
        for aa in range(A):
            for bb in range(B):
                for cc in range(2):
                    dense_t[aa, bb, :, cc * T:(cc + 1) * T] = dense[cc, bb, aa].T

    def pack(dst, top, row):
        n = top.shape[0]
        high = row.astype(BF16)
        dst[0:n, :] = top.astype(BF16)
        dst[n:n + EXTRA, 0:T] = high
        dst[n:n + EXTRA, T:2 * T] = (row - high.astype(F32)).astype(BF16)

    for cp in panel_in:
        cp.wait_recv()
    order = [2, 3, 1, 0] if A == 4 else list(range(1, A)) + [0]
    def block_sums(kb):
        bb = plus(b, kb, B)
        dense_in[kb].wait_recv()
        res = dot(dense[c, bb].reshape(A * T, R * T), panel[c])
        res = res + dot(dense_sib[bb].reshape(A * T, R * T), panel[1 - c])
        sums_by[kb] = res.reshape(A, T, hid)

    for kb in range(1, B):
        block_sums(kb)
        for ka in order:
            x_send[kb - 1, ka] = sums_by[kb, plus(a, ka, A), CUT:T].astype(BF16)
            i = (kb - 1) * A + ka
            cp = rcopy(x_send.at[kb - 1, ka], x_recv.at[kb - 1, ka], xs.at[i], xr.at[i], rep,
                       dom_of(a, plus(b, kb, B), c))
            cp.start()
            copies.append(cp)
    block_sums(0)
    for ka in order[:-1]:
        aa = plus(a, ka, A)
        for kb in range(B):
            z2_send[ka, kb * CUT:(kb + 1) * CUT, :] = sums_by[kb, aa, 0:CUT].astype(BF16)
        cp = rcopy(z2_send.at[ka], z2_recv.at[ka], z2s.at[ka], z2r.at[ka], rep, dom_of(aa, b, c))
        cp.start()
        copies.append(cp)

    def with_x(ka):
        top = sums_by[0, plus(a, ka, A), CUT:T]
        for kb in range(1, B):
            i = (kb - 1) * A + ka
            rcopy(x_send.at[kb - 1, ka], x_recv.at[kb - 1, ka], xs.at[i], xr.at[i], rep, sib).wait_recv()
            top = top + x_recv[kb - 1, ka].astype(F32)
        return top

    for ka in order[:-1]:
        z_send[ka] = with_x(ka).astype(BF16)
        cp = rcopy(z_send.at[ka], z_recv.at[ka], zs.at[ka], zr.at[ka], rep,
                   dom_of(plus(a, ka, A), b, c))
        cp.start()
        copies.append(cp)
    for ka in order[:-1]:
        rcopy(z2_send.at[ka], z2_recv.at[ka], z2s.at[ka], z2r.at[ka], rep, sib).wait_recv()
    for kb in list(range(1, B)) + [0]:
        part = sums_by[kb, a, 0:CUT]
        for ka in range(1, A):
            part = part + z2_recv[ka, kb * CUT:(kb + 1) * CUT, :].astype(F32)
        if kb > 0:
            x2_send[kb] = part.astype(BF16)
            cp = rcopy(x2_send.at[kb], x2_recv.at[kb], x2s.at[kb], x2r.at[kb], rep,
                       dom_of(a, plus(b, kb, B), c))
            cp.start()
            copies.append(cp)
    head = part
    scatter_wait(pick_f, f_in, fs, fr)
    deg = f_in[0, chunk:chunk + EXTRA].astype(F32)
    for k in range(1, n_dom):
        deg = deg + f_in[k, chunk:chunk + EXTRA].astype(F32)
    inv = 1.0 / (1.0 + (deg[0:8] + deg[8:16]))
    inv = jnp.concatenate([inv, inv], axis=0)

    def as_column(row):
        col = jnp.broadcast_to(row[0:1, :], (T, T)).T
        return jnp.concatenate([col] * (hid // T), axis=1)

    inv_col = as_column(inv)

    top = with_x(0)
    for ka in order[:-1]:
        rcopy(z_send.at[ka], z_recv.at[ka], zs.at[ka], zr.at[ka], rep, sib).wait_recv()
        top = top + z_recv[ka].astype(F32)
    for kb in range(1, B):
        rcopy(x2_send.at[kb], x2_recv.at[kb], x2s.at[kb], x2r.at[kb], rep, sib).wait_recv()
        head = head + x2_recv[kb].astype(F32)
    top = jnp.concatenate([head, top], axis=0)

    mean = (top * inv_col).astype(BF16)
    pre = pre_self + dot(mean, w_neigh_ref[...])
    g = jax.nn.sigmoid(pre)
    d_pre = (d_out_ref[...].astype(F32) * g * (1.0 + pre * (1.0 - g))).astype(BF16)
    mine = gather.at[a, b, c]
    pack(mine, d_pre, inv)

    def send_a(ka):
        cp = rcopy(mine, mine, gzs.at[ka], gzr.at[ka], rep, dom_of(plus(a, ka, A), b, c))
        cp.start()
        copies.append(cp)

    def block_at(ka, kb, cc):
        return gather.at[plus(a, A - ka, A), plus(b, B - kb, B), cc]

    def send_b(ka):
        blk = block_at(ka, 0, c)
        for kb in range(1, B):
            i = kb * A + ka
            cp = rcopy(blk, blk, gxs.at[i], gxr.at[i], rep, dom_of(a, plus(b, kb, B), c))
            cp.start()
            copies.append(cp)

    def send_c(ka, kb):
        blk = block_at(ka, kb, c)
        i = kb * A + ka
        cp = rcopy(blk, blk, gcs.at[i], gcr.at[i], rep, sib)
        cp.start()
        copies.append(cp)

    early = copies[:]
    copies.clear()
    for ka in order[:-1]:
        send_a(ka)
    send_b(0)
    send_c(0, 0)
    out_ref[...] = (pre * g).astype(BF16)
    m_t[...] = mean.T
    d_self = dot_nt(d_pre, w_self_ref[...])
    for ec in early:
        ec.wait_send()
    panel_acc[...] = jnp.zeros_like(panel_acc)
    grad_acc[...] = jnp.zeros_like(grad_acc)
    scatter(pick_m, m_in, ms, mr)
    m_in[dom] = m_t[chunk_at(dom), :]

    def use(ka, kbs):
        d, cols, lhs = [], [], []
        aa = plus(a, A - ka, A)
        for kb in kbs:
            bb = plus(b, B - kb, B)
            blk = block_at(ka, kb, 1 - c)
            i = kb * A + ka
            rcopy(blk, blk, gcs.at[i], gcr.at[i], rep, sib).wait_recv()
            for cc in range(2):
                d.append(gather[aa, bb, cc, 0:T, :])
                row = gather[aa, bb, cc, T:T + EXTRA, :].astype(F32)
                cols.append(as_column(row[:, 0:T] + row[:, T:2 * T]))
            if small:
                lhs.append(dense_t[aa, bb])
        d_sum = dot(jnp.concatenate(d, axis=0), w_neigh_t[...]) * jnp.concatenate(cols, axis=0)
        d_sum = d_sum.astype(BF16)
        if small:
            panel_acc[...] += dot(jnp.concatenate(lhs, axis=1), d_sum)
            return
        for n, kb in enumerate(kbs):
            bb = plus(b, B - kb, B)
            for cc in range(2):
                at = (n * 2 + cc) * T
                for s in range(R):
                    panel_acc[s * T:(s + 1) * T, :] += dot_tn(
                        dense[cc, bb, aa, :, s * T:(s + 1) * T], d_sum[at:at + T]
                    )

    def grads_of(pairs):
        lhs, rhs = [], []
        for ka, kb in pairs:
            aa, bb = plus(a, A - ka, A), plus(b, B - kb, B)
            for cc in range(2):
                at = dom_of(aa, bb, cc)
                lhs.append(jnp.concatenate([f_in[at, 0:chunk], m_in[at]], axis=0))
                rhs.append(gather[aa, bb, cc, 0:T, :])
        grad_acc[...] += dot(jnp.concatenate(lhs, axis=1), jnp.concatenate(rhs, axis=0))

    done = []
    later = []
    for ka in [0] + order[:-1]:
        if ka > 0:
            blk = block_at(ka, 0, c)
            rcopy(blk, blk, gzs.at[ka], gzr.at[ka], rep, sib).wait_recv()
            send_b(ka)
            send_c(ka, 0)
        for kb in range(1, B):
            blk = block_at(ka, kb, c)
            i = kb * A + ka
            rcopy(blk, blk, gxs.at[i], gxr.at[i], rep, sib).wait_recv()
            send_c(ka, kb)
        if later:
            use(later[0][0], [kb for _, kb in later])
        done += later
        later = [(ka, kb) for kb in range(B)]
    use(later[0][0], [later[0][1]])
    done.append(later.pop(0))
    scatter_wait(pick_m, m_in, ms, mr)
    grads_of(done)
    for ka, kb in later:
        use(ka, [kb])

    back = []
    for kr in range(1, R):
        to = plus(rep, kr, R)
        rows = pl.ds(pl.multiple_of(to * T, T), T)
        back_send[kr] = panel_acc[rows, :].astype(BF16)
        cp = rcopy(back_send.at[kr], back_recv.at[kr], bs.at[kr], br.at[kr], to, dom)
        cp.start()
        back.append(cp)
    if later:
        grads_of(later)
    gr_send[...] = grad_acc[...]
    for kr in range(1, R):
        cp = rcopy(gr_send, gr_recv.at[kr], grs.at[kr], grr.at[kr], plus(rep, kr, R), dom)
        cp.start()
        back.append(cp)
    for cp in copies:
        cp.wait_send()

    mine_rows = pl.ds(pl.multiple_of(rep * T, T), T)
    total = d_self + panel_acc[mine_rows, :]
    for kr in range(1, R):
        back[kr - 1].wait_recv()
        total = total + back_recv[kr].astype(F32)
    d_feats_ref[...] = total.astype(BF16)
    grads = grad_acc[...]
    for kr in range(1, R):
        back[R - 1 + kr - 1].wait_recv()
        grads = grads + gr_recv[kr]
    at = lax.rem(dom * share, chunk)
    for i, ref in enumerate((g_self_ref, g_neigh_ref)):
        part = grads[i * chunk:(i + 1) * chunk]
        res = part[0:share]
        for k in range(1, chunk // share):
            res = jnp.where(at == k * share, part[k * share:(k + 1) * share], res)
        ref[...] = res

    for cp in back:
        cp.wait_send()


def finish(*refs):
    n = (len(refs) - 1) // 2
    sems = refs[-1]
    moves = [pltpu.make_async_copy(refs[i], refs[n + i], sems.at[i]) for i in range(n)]
    for cp in moves:
        cp.start()
    for cp in moves:
        cp.wait()


def per_device(feats, w_self, w_neigh, tile_vals, tile_owner, tile_src, tile_count, d_out):
    R = lax.axis_size("rep")
    n_dom = lax.axis_size("dom")
    A = 4
    B = n_dom // (2 * A)
    T, hid = feats.shape
    tiles = tile_vals.shape[2]
    share = hid // n_dom
    chunk = max(share, 16)
    small = tiles <= 16
    msg = T + EXTRA
    dims = (R, A, B, T, hid, tiles, share, chunk, small)
    vmem = pl.BlockSpec(memory_space=pltpu.VMEM)
    anywhere = pl.BlockSpec(memory_space=pl.ANY)
    dma = pltpu.SemaphoreType.DMA
    scratch = [
        pltpu.VMEM((T, hid), BF16),
        pltpu.VMEM((hid, hid), BF16),
        pltpu.VMEM((hid, hid), BF16),
        pltpu.VMEM((tiles, T, T), BF16),
        pltpu.SMEM((tiles,), jnp.int32),
        pltpu.SMEM((tiles,), jnp.int32),
        pltpu.SMEM((1, 1), jnp.int32),
        pltpu.VMEM((T, hid), BF16),
        dma((8,)),
        pltpu.VMEM((2, R * T, hid), BF16),
        pltpu.VMEM((2, B, A, T, R * T), BF16),
        pltpu.VMEM((B, A, T, R * T), BF16),
        pltpu.VMEM((A, B, R * T, 2 * T) if small else (1, 1, 16, 128), BF16),
        pltpu.VMEM((B - 1, A, T - CUT, hid), BF16),
        pltpu.VMEM((B - 1, A, T - CUT, hid), BF16),
        pltpu.VMEM((B, A, T, hid), F32),
        pltpu.VMEM((A, T - CUT, hid), BF16),
        pltpu.VMEM((A, T - CUT, hid), BF16),
        pltpu.VMEM((A, B * CUT, hid), BF16),
        pltpu.VMEM((A, B * CUT, hid), BF16),
        pltpu.VMEM((B, CUT, hid), BF16),
        pltpu.VMEM((B, CUT, hid), BF16),
        pltpu.VMEM((A, B, 2, msg, hid), BF16),
        pltpu.VMEM((hid, T), BF16),
        pltpu.VMEM((hid, T), BF16),
        pltpu.VMEM((tiles, 8, T), F32),
        pltpu.VMEM((n_dom, chunk + EXTRA, T), BF16),
        pltpu.VMEM((n_dom, chunk + EXTRA, T), BF16),
        pltpu.VMEM((n_dom, chunk, T), BF16),
        pltpu.VMEM((hid, hid), BF16),
        pltpu.VMEM((2 * chunk, hid), F32),
        pltpu.VMEM((R * T, hid), F32),
        pltpu.VMEM((R, T, hid), BF16),
        pltpu.VMEM((R, T, hid), BF16),
        pltpu.VMEM((2 * chunk, hid), F32),
        pltpu.VMEM((R, 2 * chunk, hid), F32),
        dma((2 * R,)), dma((2 * R,)),
        dma((B,)), dma((B,)),
        dma(((B - 1) * A,)), dma(((B - 1) * A,)),
        dma((A,)), dma((A,)),
        dma((A,)), dma((A,)),
        dma((B,)), dma((B,)),
        dma((A,)), dma((A,)),
        dma((A * B,)), dma((A * B,)),
        dma((A * B,)), dma((A * B,)),
        dma((n_dom,)), dma((n_dom,)),
        dma((n_dom,)), dma((n_dom,)),
        dma((R,)), dma((R,)),
        dma((R,)), dma((R,)),
    ]
    results = pl.pallas_call(
        functools.partial(kernel, dims),
        out_shape=(
            pltpu.VMEM((T, hid), BF16),
            pltpu.VMEM((T, hid), BF16),
            pltpu.VMEM((share, hid), F32),
            pltpu.VMEM((share, hid), F32),
        ),
        in_specs=[anywhere] * 8,
        out_specs=(vmem, vmem, vmem, vmem),
        scratch_shapes=scratch,
        compiler_params=pltpu.CompilerParams(
            collective_id=0, has_side_effects=True, vmem_limit_bytes=60 * 1024 * 1024
        ),
        name="sage_layer",
    )(
        feats, w_self, w_neigh, tile_vals[0, 0], tile_owner.reshape(-1), tile_src.reshape(-1),
        tile_count, d_out,
    )
    return pl.pallas_call(
        finish,
        out_shape=tuple(jax.ShapeDtypeStruct(r.shape, r.dtype) for r in results),
        in_specs=[vmem] * 4,
        out_specs=(anywhere,) * 4,
        scratch_shapes=[dma((4,))],
        compiler_params=pltpu.CompilerParams(vmem_limit_bytes=1024 * 1024),
        name="place_results",
    )(*results)


def solution(mesh):
    in_specs = (
        P(("rep", "dom"), None),
        P(),
        P(),
        P("rep", "dom", None, None, None),
        P("rep", "dom", None),
        P("rep", "dom", None),
        P("rep", "dom"),
        P(("rep", "dom"), None),
    )
    out_specs = (P(("rep", "dom"), None), P(("rep", "dom"), None), P("dom", None), P("dom", None))
    return jax.shard_map(
        per_device, mesh=mesh, in_specs=in_specs, out_specs=out_specs, check_vma=False
    )
```

```python
import functools

import jax
import jax.numpy as jnp
from jax import lax
from jax.experimental import pallas as pl
from jax.experimental.pallas import tpu as pltpu
from jax.sharding import PartitionSpec as P

F32 = jnp.float32
BF16 = jnp.bfloat16
MESH = pl.DeviceIdType.MESH
CUT = 48
EXTRA = 16


def dot(x, y):
    return jnp.dot(x, y, preferred_element_type=F32)


def dot_nt(x, y):
    return lax.dot_general(x, y, (((1,), (1,)), ((), ())), preferred_element_type=F32)


def dot_tn(x, y):
    return lax.dot_general(x, y, (((0,), (0,)), ((), ())), preferred_element_type=F32)


def kernel(
    dims,
    feats_in, w_self_in, w_neigh_in, tiles_in, owner_in, src_in, count_in, d_out_in,
    out_ref, d_feats_ref, g_self_ref, g_neigh_ref,
    feats_ref, w_self_ref, w_neigh_ref, tiles_ref, owner_ref, src_ref, count_ref, d_out_ref, load_s,
    panel, dense, dense_sib, dense_t, x_send, x_recv, sums_by, z_send, z_recv, z2_send, z2_recv, x2_send, x2_recv,
    gather, f_t, m_t, row_sums, f_send, f_in, m_in, w_neigh_t, grad_acc, panel_acc, back_send, back_recv,
    gr_send, gr_recv,
    panel_s, panel_r, dense_s, dense_r, xs, xr, zs, zr, z2s, z2r, x2s, x2r, gzs, gzr, gxs, gxr, gcs, gcr,
    fs, fr, ms, mr, bs, br, grs, grr,
):
    R, A, B, T, hid, tiles, share, chunk, small = dims
    n_dom = A * B * 2
    rep = lax.axis_index("rep")
    dom = lax.axis_index("dom")
    c = lax.rem(dom, 2)
    b = lax.rem(lax.div(dom, 2), B)
    a = lax.div(dom, 2 * B)

    def dom_of(aa, bb, cc):
        return (aa * B + bb) * 2 + cc

    def plus(x, k, n):
        return lax.rem(x + k, n)

    sib = dom_of(a, b, 1 - c)

    def rcopy(src, dst, s, r, to_rep, to_dom):
        return pltpu.make_async_remote_copy(
            src_ref=src, dst_ref=dst, send_sem=s, recv_sem=r,
            device_id=(to_rep, to_dom), device_id_type=MESH,
        )

    barrier = pltpu.get_barrier_semaphore()
    for k in range(1, n_dom):
        pl.semaphore_signal(barrier, inc=1, device_id=(rep, plus(dom, k, n_dom)), device_id_type=MESH)
    for k in range(1, R):
        for cc in range(2):
            pl.semaphore_signal(
                barrier, inc=1, device_id=(plus(rep, k, R), dom_of(a, b, cc)), device_id_type=MESH
            )

    loads = []
    for i, (src, dst) in enumerate((
        (count_in, count_ref), (owner_in, owner_ref), (src_in, src_ref), (tiles_in, tiles_ref),
        (feats_in, feats_ref), (w_self_in, w_self_ref), (w_neigh_in, w_neigh_ref),
        (d_out_in, d_out_ref),
    )):
        cp = pltpu.make_async_copy(src, dst, load_s.at[i])
        cp.start()
        loads.append(cp)
    loads[4].wait()
    pl.semaphore_wait(barrier, n_dom - 1 + 2 * (R - 1))

    copies = []
    panel_in = []
    for kr in range(R):
        for kc in range(2):
            if kr == 0 and kc == 0:
                continue
            to_c = plus(c, kc, 2)
            cp = rcopy(
                feats_ref, panel.at[c, pl.ds(pl.multiple_of(rep * T, T), T)],
                panel_s.at[kr * 2 + kc], panel_r.at[kr * 2 + kc], plus(rep, R - kr, R),
                dom_of(a, b, to_c),
            )
            cp.start()
            copies.append(cp)
            panel_in.append(cp)
    for cp in loads[:4]:
        cp.wait()

    keys = None
    if small:
        keys = [
            jnp.where(t < count_ref[0, 0], owner_ref[t] * R + src_ref[t], -1) for t in range(tiles)
        ]

    def place(pair):
        if small:
            at, live = jnp.int32(0), jnp.int32(0)
            for t in range(tiles):
                hit = keys[t] == pair
                at = jnp.where(hit, t, at)
                live = jnp.where(hit, 1, live)
            return at, live

        def look(t, state):
            hit = (owner_ref[t] * R + src_ref[t] == pair) & (t < count_ref[0, 0])
            return jnp.where(hit, t, state[0]), jnp.where(hit, 1, state[1])

        return lax.fori_loop(0, tiles, look, (jnp.int32(0), jnp.int32(0)))

    if small:
        sums = dot_nt(jnp.ones((EXTRA, T), BF16), tiles_ref[...].reshape(tiles * T, T))
        for t in range(tiles):
            row_sums[t] = sums[0:8, t * T:(t + 1) * T]
    else:
        def sum_tile(t, _):
            row_sums[t] = dot_nt(jnp.ones((EXTRA, T), BF16), tiles_ref[t])[0:8]
            return 0
        lax.fori_loop(0, tiles, sum_tile, 0)

    def build(cc, bb):
        def one(aa, _):
            d = dom_of(aa, bb, cc)
            for s in range(R):
                at, live = place(d * R + s)
                mask = jnp.full((T, T), live.astype(F32), F32).astype(BF16)
                dense[cc, bb, aa, :, s * T:(s + 1) * T] = tiles_ref[at] * mask
                part = row_sums[at] * live.astype(F32)
                deg = part if s == 0 else deg + part
            high = deg.astype(BF16).astype(F32)
            f_send[d, chunk:chunk + EXTRA, :] = jnp.concatenate([high, deg - high], axis=0).astype(BF16)
            return 0
        if small:
            for aa in range(A):
                one(aa, 0)
        else:
            lax.fori_loop(0, A, one, 0)

    for kb in list(range(1, B)) + [0]:
        build(1 - c, plus(b, kb, B))

    for cp in loads[5:]:
        cp.wait()
    f_t[...] = feats_ref[...].T
    for d in range(n_dom):
        row = d * share // chunk * chunk
        f_send[d, 0:chunk, :] = f_t[row:row + chunk, :]
    panel[c, pl.ds(pl.multiple_of(rep * T, T), T), :] = feats_ref[...]

    dense_in = {}
    for kb in list(range(1, B)) + [0]:
        bb = plus(b, kb, B)
        cp = rcopy(dense.at[1 - c, bb], dense_sib.at[bb], dense_s.at[kb], dense_r.at[kb], rep, sib)
        cp.start()
        copies.append(cp)
        dense_in[kb] = cp

    def chunk_at(d):
        return pl.ds(pl.multiple_of(lax.div(d * share, chunk) * chunk, chunk), chunk)

    def scatter(pick, dst, s, r):
        for k in range(1, n_dom):
            to = plus(dom, k, n_dom)
            cp = rcopy(pick(to), dst.at[dom], s.at[k], r.at[k], rep, to)
            cp.start()
            copies.append(cp)

    def scatter_wait(pick, dst, s, r):
        for k in range(1, n_dom):
            frm = plus(dom, n_dom - k, n_dom)
            rcopy(pick(frm), dst.at[frm], s.at[k], r.at[k], rep, frm).wait_recv()

    def pick_f(d):
        return f_send.at[d]

    def pick_m(d):
        return m_t.at[chunk_at(d)]

    for kb in list(range(1, B)) + [0]:
        build(c, plus(b, kb, B))
    scatter(pick_f, f_in, fs, fr)
    f_in[dom] = f_send[dom]

    w_neigh_t[...] = w_neigh_ref[...].T
    pre_self = dot(feats_ref[...], w_self_ref[...])
    if small:
        for aa in range(A):
            for bb in range(B):
                for cc in range(2):
                    dense_t[aa, bb, :, cc * T:(cc + 1) * T] = dense[cc, bb, aa].T

    def pack(dst, top, row):
        n = top.shape[0]
        high = row.astype(BF16)
        dst[0:n, :] = top.astype(BF16)
        dst[n:n + EXTRA, 0:T] = high
        dst[n:n + EXTRA, T:2 * T] = (row - high.astype(F32)).astype(BF16)

    for cp in panel_in:
        cp.wait_recv()
    order = [2, 3, 1, 0] if A == 4 else list(range(1, A)) + [0]
    def block_sums(kb):
        bb = plus(b, kb, B)
        dense_in[kb].wait_recv()
        res = dot(dense[c, bb].reshape(A * T, R * T), panel[c])
        res = res + dot(dense_sib[bb].reshape(A * T, R * T), panel[1 - c])
        sums_by[kb] = res.reshape(A, T, hid)

    for kb in range(1, B):
        block_sums(kb)
        for ka in order:
            x_send[kb - 1, ka] = sums_by[kb, plus(a, ka, A), CUT:T].astype(BF16)
            i = (kb - 1) * A + ka
            cp = rcopy(x_send.at[kb - 1, ka], x_recv.at[kb - 1, ka], xs.at[i], xr.at[i], rep,
                       dom_of(a, plus(b, kb, B), c))
            cp.start()
            copies.append(cp)
    block_sums(0)
    for ka in order[:-1]:
        aa = plus(a, ka, A)
        for kb in range(B):
            z2_send[ka, kb * CUT:(kb + 1) * CUT, :] = sums_by[kb, aa, 0:CUT].astype(BF16)
        cp = rcopy(z2_send.at[ka], z2_recv.at[ka], z2s.at[ka], z2r.at[ka], rep, dom_of(aa, b, c))
        cp.start()
        copies.append(cp)

    def with_x(ka):
        top = sums_by[0, plus(a, ka, A), CUT:T]
        for kb in range(1, B):
            i = (kb - 1) * A + ka
            rcopy(x_send.at[kb - 1, ka], x_recv.at[kb - 1, ka], xs.at[i], xr.at[i], rep, sib).wait_recv()
            top = top + x_recv[kb - 1, ka].astype(F32)
        return top

    for ka in order[:-1]:
        z_send[ka] = with_x(ka).astype(BF16)
        cp = rcopy(z_send.at[ka], z_recv.at[ka], zs.at[ka], zr.at[ka], rep,
                   dom_of(plus(a, ka, A), b, c))
        cp.start()
        copies.append(cp)
    for ka in order[:-1]:
        rcopy(z2_send.at[ka], z2_recv.at[ka], z2s.at[ka], z2r.at[ka], rep, sib).wait_recv()
    for kb in list(range(1, B)) + [0]:
        part = sums_by[kb, a, 0:CUT]
        for ka in range(1, A):
            part = part + z2_recv[ka, kb * CUT:(kb + 1) * CUT, :].astype(F32)
        if kb > 0:
            x2_send[kb] = part.astype(BF16)
            cp = rcopy(x2_send.at[kb], x2_recv.at[kb], x2s.at[kb], x2r.at[kb], rep,
                       dom_of(a, plus(b, kb, B), c))
            cp.start()
            copies.append(cp)
    head = part
    scatter_wait(pick_f, f_in, fs, fr)
    deg = f_in[0, chunk:chunk + EXTRA].astype(F32)
    for k in range(1, n_dom):
        deg = deg + f_in[k, chunk:chunk + EXTRA].astype(F32)
    inv = 1.0 / (1.0 + (deg[0:8] + deg[8:16]))
    inv = jnp.concatenate([inv, inv], axis=0)

    def as_column(row):
        col = jnp.broadcast_to(row[0:1, :], (T, T)).T
        return jnp.concatenate([col] * (hid // T), axis=1)

    inv_col = as_column(inv)

    top = with_x(0)
    for ka in order[:-1]:
        rcopy(z_send.at[ka], z_recv.at[ka], zs.at[ka], zr.at[ka], rep, sib).wait_recv()
        top = top + z_recv[ka].astype(F32)
    for kb in range(1, B):
        rcopy(x2_send.at[kb], x2_recv.at[kb], x2s.at[kb], x2r.at[kb], rep, sib).wait_recv()
        head = head + x2_recv[kb].astype(F32)
    top = jnp.concatenate([head, top], axis=0)

    mean = (top * inv_col).astype(BF16)
    pre = pre_self + dot(mean, w_neigh_ref[...])
    g = jax.nn.sigmoid(pre)
    d_pre = (d_out_ref[...].astype(F32) * g * (1.0 + pre * (1.0 - g))).astype(BF16)
    mine = gather.at[a, b, c]
    pack(mine, d_pre, inv)

    def send_a(ka):
        cp = rcopy(mine, mine, gzs.at[ka], gzr.at[ka], rep, dom_of(plus(a, ka, A), b, c))
        cp.start()
        copies.append(cp)

    def block_at(ka, kb, cc):
        return gather.at[plus(a, A - ka, A), plus(b, B - kb, B), cc]

    def send_b(ka):
        blk = block_at(ka, 0, c)
        for kb in range(1, B):
            i = kb * A + ka
            cp = rcopy(blk, blk, gxs.at[i], gxr.at[i], rep, dom_of(a, plus(b, kb, B), c))
            cp.start()
            copies.append(cp)

    def send_c(ka, kb):
        blk = block_at(ka, kb, c)
        i = kb * A + ka
        cp = rcopy(blk, blk, gcs.at[i], gcr.at[i], rep, sib)
        cp.start()
        copies.append(cp)

    early = copies[:]
    copies.clear()
    for ka in order[:-1]:
        send_a(ka)
    send_b(0)
    send_c(0, 0)
    out_ref[...] = (pre * g).astype(BF16)
    m_t[...] = mean.T
    d_self = dot_nt(d_pre, w_self_ref[...])
    for ec in early:
        ec.wait_send()
    panel_acc[...] = jnp.zeros_like(panel_acc)
    grad_acc[...] = jnp.zeros_like(grad_acc)
    scatter(pick_m, m_in, ms, mr)
    m_in[dom] = m_t[chunk_at(dom), :]

    def use(ka, kbs):
        d, cols, lhs = [], [], []
        aa = plus(a, A - ka, A)
        for kb in kbs:
            bb = plus(b, B - kb, B)
            blk = block_at(ka, kb, 1 - c)
            i = kb * A + ka
            rcopy(blk, blk, gcs.at[i], gcr.at[i], rep, sib).wait_recv()
            for cc in range(2):
                d.append(gather[aa, bb, cc, 0:T, :])
                row = gather[aa, bb, cc, T:T + EXTRA, :].astype(F32)
                cols.append(as_column(row[:, 0:T] + row[:, T:2 * T]))
            if small:
                lhs.append(dense_t[aa, bb])
        d_sum = dot(jnp.concatenate(d, axis=0), w_neigh_t[...]) * jnp.concatenate(cols, axis=0)
        d_sum = d_sum.astype(BF16)
        if small:
            panel_acc[...] += dot(jnp.concatenate(lhs, axis=1), d_sum)
            return
        for n, kb in enumerate(kbs):
            bb = plus(b, B - kb, B)
            for cc in range(2):
                at = (n * 2 + cc) * T
                for s in range(R):
                    panel_acc[s * T:(s + 1) * T, :] += dot_tn(
                        dense[cc, bb, aa, :, s * T:(s + 1) * T], d_sum[at:at + T]
                    )

    def grads_of(pairs):
        lhs, rhs = [], []
        for ka, kb in pairs:
            aa, bb = plus(a, A - ka, A), plus(b, B - kb, B)
            for cc in range(2):
                at = dom_of(aa, bb, cc)
                lhs.append(jnp.concatenate([f_in[at, 0:chunk], m_in[at]], axis=0))
                rhs.append(gather[aa, bb, cc, 0:T, :])
        grad_acc[...] += dot(jnp.concatenate(lhs, axis=1), jnp.concatenate(rhs, axis=0))

    def pass_a(ka):
        blk = block_at(ka, 0, c)
        rcopy(blk, blk, gzs.at[ka], gzr.at[ka], rep, sib).wait_recv()
        send_b(ka)
        send_c(ka, 0)

    def pass_b(ka):
        for kb in range(1, B):
            blk = block_at(ka, kb, c)
            i = kb * A + ka
            rcopy(blk, blk, gxs.at[i], gxr.at[i], rep, sib).wait_recv()
            send_c(ka, kb)

    every = list(range(B))
    line = [0] + order[:-1]
    pass_b(0)
    for ka in line[1:]:
        pass_a(ka)
    for n in range(A - 1):
        pass_b(line[n + 1])
        use(line[n], every)
    done = [(ka, kb) for ka in line[:-1] for kb in every]
    later = [(line[-1], kb) for kb in every]
    use(later[0][0], [later[0][1]])
    done.append(later.pop(0))
    scatter_wait(pick_m, m_in, ms, mr)
    grads_of(done)
    for ka, kb in later:
        use(ka, [kb])

    back = []
    for kr in range(1, R):
        to = plus(rep, kr, R)
        rows = pl.ds(pl.multiple_of(to * T, T), T)
        back_send[kr] = panel_acc[rows, :].astype(BF16)
        cp = rcopy(back_send.at[kr], back_recv.at[kr], bs.at[kr], br.at[kr], to, dom)
        cp.start()
        back.append(cp)
    if later:
        grads_of(later)
    gr_send[...] = grad_acc[...]
    for kr in range(1, R):
        cp = rcopy(gr_send, gr_recv.at[kr], grs.at[kr], grr.at[kr], plus(rep, kr, R), dom)
        cp.start()
        back.append(cp)
    for cp in copies:
        cp.wait_send()

    mine_rows = pl.ds(pl.multiple_of(rep * T, T), T)
    total = d_self + panel_acc[mine_rows, :]
    for kr in range(1, R):
        back[kr - 1].wait_recv()
        total = total + back_recv[kr].astype(F32)
    d_feats_ref[...] = total.astype(BF16)
    grads = grad_acc[...]
    for kr in range(1, R):
        back[R - 1 + kr - 1].wait_recv()
        grads = grads + gr_recv[kr]
    at = lax.rem(dom * share, chunk)
    for i, ref in enumerate((g_self_ref, g_neigh_ref)):
        part = grads[i * chunk:(i + 1) * chunk]
        res = part[0:share]
        for k in range(1, chunk // share):
            res = jnp.where(at == k * share, part[k * share:(k + 1) * share], res)
        ref[...] = res

    for cp in back:
        cp.wait_send()


def finish(*refs):
    n = (len(refs) - 1) // 2
    sems = refs[-1]
    moves = [pltpu.make_async_copy(refs[i], refs[n + i], sems.at[i]) for i in range(n)]
    for cp in moves:
        cp.start()
    for cp in moves:
        cp.wait()


def per_device(feats, w_self, w_neigh, tile_vals, tile_owner, tile_src, tile_count, d_out):
    R = lax.axis_size("rep")
    n_dom = lax.axis_size("dom")
    A = 4
    B = n_dom // (2 * A)
    T, hid = feats.shape
    tiles = tile_vals.shape[2]
    share = hid // n_dom
    chunk = max(share, 16)
    small = tiles <= 16
    msg = T + EXTRA
    dims = (R, A, B, T, hid, tiles, share, chunk, small)
    vmem = pl.BlockSpec(memory_space=pltpu.VMEM)
    anywhere = pl.BlockSpec(memory_space=pl.ANY)
    dma = pltpu.SemaphoreType.DMA
    scratch = [
        pltpu.VMEM((T, hid), BF16),
        pltpu.VMEM((hid, hid), BF16),
        pltpu.VMEM((hid, hid), BF16),
        pltpu.VMEM((tiles, T, T), BF16),
        pltpu.SMEM((tiles,), jnp.int32),
        pltpu.SMEM((tiles,), jnp.int32),
        pltpu.SMEM((1, 1), jnp.int32),
        pltpu.VMEM((T, hid), BF16),
        dma((8,)),
        pltpu.VMEM((2, R * T, hid), BF16),
        pltpu.VMEM((2, B, A, T, R * T), BF16),
        pltpu.VMEM((B, A, T, R * T), BF16),
        pltpu.VMEM((A, B, R * T, 2 * T) if small else (1, 1, 16, 128), BF16),
        pltpu.VMEM((B - 1, A, T - CUT, hid), BF16),
        pltpu.VMEM((B - 1, A, T - CUT, hid), BF16),
        pltpu.VMEM((B, A, T, hid), F32),
        pltpu.VMEM((A, T - CUT, hid), BF16),
        pltpu.VMEM((A, T - CUT, hid), BF16),
        pltpu.VMEM((A, B * CUT, hid), BF16),
        pltpu.VMEM((A, B * CUT, hid), BF16),
        pltpu.VMEM((B, CUT, hid), BF16),
        pltpu.VMEM((B, CUT, hid), BF16),
        pltpu.VMEM((A, B, 2, msg, hid), BF16),
        pltpu.VMEM((hid, T), BF16),
        pltpu.VMEM((hid, T), BF16),
        pltpu.VMEM((tiles, 8, T), F32),
        pltpu.VMEM((n_dom, chunk + EXTRA, T), BF16),
        pltpu.VMEM((n_dom, chunk + EXTRA, T), BF16),
        pltpu.VMEM((n_dom, chunk, T), BF16),
        pltpu.VMEM((hid, hid), BF16),
        pltpu.VMEM((2 * chunk, hid), F32),
        pltpu.VMEM((R * T, hid), F32),
        pltpu.VMEM((R, T, hid), BF16),
        pltpu.VMEM((R, T, hid), BF16),
        pltpu.VMEM((2 * chunk, hid), F32),
        pltpu.VMEM((R, 2 * chunk, hid), F32),
        dma((2 * R,)), dma((2 * R,)),
        dma((B,)), dma((B,)),
        dma(((B - 1) * A,)), dma(((B - 1) * A,)),
        dma((A,)), dma((A,)),
        dma((A,)), dma((A,)),
        dma((B,)), dma((B,)),
        dma((A,)), dma((A,)),
        dma((A * B,)), dma((A * B,)),
        dma((A * B,)), dma((A * B,)),
        dma((n_dom,)), dma((n_dom,)),
        dma((n_dom,)), dma((n_dom,)),
        dma((R,)), dma((R,)),
        dma((R,)), dma((R,)),
    ]
    results = pl.pallas_call(
        functools.partial(kernel, dims),
        out_shape=(
            pltpu.VMEM((T, hid), BF16),
            pltpu.VMEM((T, hid), BF16),
            pltpu.VMEM((share, hid), F32),
            pltpu.VMEM((share, hid), F32),
        ),
        in_specs=[anywhere] * 8,
        out_specs=(vmem, vmem, vmem, vmem),
        scratch_shapes=scratch,
        compiler_params=pltpu.CompilerParams(
            collective_id=0, has_side_effects=True, vmem_limit_bytes=60 * 1024 * 1024
        ),
        name="sage_layer",
    )(
        feats, w_self, w_neigh, tile_vals[0, 0], tile_owner.reshape(-1), tile_src.reshape(-1),
        tile_count, d_out,
    )
    return pl.pallas_call(
        finish,
        out_shape=tuple(jax.ShapeDtypeStruct(r.shape, r.dtype) for r in results),
        in_specs=[vmem] * 4,
        out_specs=(anywhere,) * 4,
        scratch_shapes=[dma((4,))],
        compiler_params=pltpu.CompilerParams(vmem_limit_bytes=1024 * 1024),
        name="place_results",
    )(*results)


def solution(mesh):
    in_specs = (
        P(("rep", "dom"), None),
        P(),
        P(),
        P("rep", "dom", None, None, None),
        P("rep", "dom", None),
        P("rep", "dom", None),
        P("rep", "dom"),
        P(("rep", "dom"), None),
    )
    out_specs = (P(("rep", "dom"), None), P(("rep", "dom"), None), P("dom", None), P("dom", None))
    return jax.shard_map(
        per_device, mesh=mesh, in_specs=in_specs, out_specs=out_specs, check_vma=False
    )
```
